128 devices in a mesh: section: 2 (over y_hi), shard: 8 (over x, core), replica: 8 (over z, y_lo).
Axes of the slice: x: 4, y: 4 (y_hi: 2, y_lo: 2; y = y_hi * 2 + y_lo), z: 4, core: 2. Of those that a mesh axis runs over, the one named last changes fastest.
Arguments:
- boundary: bfloat16 [2, 2, 8, 768, 1024], P('section', None, 'replica', 'shard'), may hold values from -6 to 6
- image_of_token: int32 [2, 8, 768], P(None, 'replica'), may hold values from 0 to 2, as said below
- ln1_gain: bfloat16 [2, 1024], P('section', 'shard'), may hold values from 0.5 to 1.5
- ln1_bias: bfloat16 [2, 1024], P('section', 'shard'), may hold values from -1.25 to 1.25
- w_qkv: bfloat16 [2, 1024, 3072], P('section', 'shard'), may hold values from -0.1875 to 0.1875
- qv_bias: bfloat16 [2, 2048], P('section', 'shard'), may hold values from -1.25 to 1.25
- w_out: bfloat16 [2, 1024, 1024], P('section', 'shard'), may hold values from -3 to 3
- out_bias: bfloat16 [2, 1024], P('section', 'shard'), may hold values from -1.25 to 1.25
- ln2_gain: bfloat16 [2, 1024], P('section', 'shard'), may hold values from 0.5 to 1.5
- ln2_bias: bfloat16 [2, 1024], P('section', 'shard'), may hold values from -1.25 to 1.25
- w_fc1: bfloat16 [2, 1024, 4096], P('section', 'shard'), may hold values from -0.1875 to 0.1875
- fc1_bias: bfloat16 [2, 4096], P('section', 'shard'), may hold values from -1.25 to 1.25
- w_fc2: bfloat16 [2, 4096, 1024], P('section', 'shard'), may hold values from -0.09375 to 0.09375
- fc2_bias: bfloat16 [2, 1024], P('section', 'shard'), may hold values from -1.25 to 1.25
Outputs:
- boundary_out: float32 [2, 2, 8, 768, 1024], P('section', None, 'replica', 'shard')
- grad_ln1_gain: float32 [2, 1024], P('section', 'shard')
- grad_ln1_bias: float32 [2, 1024], P('section', 'shard')
- grad_w_qkv: float32 [2, 1024, 3072], P('section', 'shard')
- grad_qv_bias: float32 [2, 2048], P('section', 'shard')
- grad_w_out: float32 [2, 1024, 1024], P('section', 'shard')
- grad_out_bias: float32 [2, 1024], P('section', 'shard')
- grad_ln2_gain: float32 [2, 1024], P('section', 'shard')
- grad_ln2_bias: float32 [2, 1024], P('section', 'shard')
- grad_w_fc1: float32 [2, 1024, 4096], P('section', 'shard')
- grad_fc1_bias: float32 [2, 4096], P('section', 'shard')
- grad_w_fc2: float32 [2, 4096, 1024], P('section', 'shard')
- grad_fc2_bias: float32 [2, 1024], P('section', 'shard')
The draws below stay inside these ranges and needn't reach their ends.
Inputs may be any that keep to these rules, and one draw needn't show every extreme that they name: `image_of_token`: in every pack the image numbers start at 0, never fall and rise by one at each new image; every image of a pack but its first and its last has exactly 577 tokens, and those two have 1 to 577 tokens.
All inputs are finite; a program needn't handle non-finite values.
Results may differ from the reference program's by a relative error of at most 0.014.
Values may be sent and summed in bfloat16 or wider, within the bound.
A program may use at most 192 MiB of HBM per device.

```python
import math
import jax
import jax.numpy as jnp
from jax import lax

D = 1024
HEADS = 16
HEAD = 64
FF = 4096
IMAGE = 577
PACK = 768
MICRO = 2
N_SECTION = 2
N_REPLICA = 8


def draw_image_of_token(key, part):
    key = jax.random.fold_in(key, 11)
    offset = jax.random.randint(key, (MICRO, N_REPLICA, 1), 0, IMAGE)
    offset = offset.at[0, 0, 0].set(IMAGE - 1)
    position = jnp.arange(PACK, dtype=jnp.int32)[None, None, :]
    return ((position + offset) // IMAGE).astype(jnp.int32)


def level_of(rng, dims, cuts, least, largest):
    loudness, own = 1.0, jax.random.fold_in(rng, 6)
    for dim, blocks in cuts:
        steps = jnp.exp(jax.random.uniform(jax.random.fold_in(own, dim), (blocks,), jnp.float32, least / len(cuts), largest / len(cuts)))
        loudness = loudness * jnp.repeat(steps, dims[dim] // blocks).reshape([-1 if axis == dim else 1 for axis in range(len(dims))])
    return loudness


def bell_draw(key, shape, scale, bound, cuts=(), kind=jnp.bfloat16):
    result = jax.random.normal(key, shape, jnp.float32) * scale
    if len(cuts) > 0:
        result = level_of(key, shape, cuts, -0.22, 0.18) * result
    return jnp.clip(result, min=-bound, max=bound).astype(kind)


def setup_inputs(seed: int = 0) -> dict:
    splits = jax.random.split(jax.random.key(seed), 15)
    boundary = bell_draw(splits[0], (N_SECTION, MICRO, N_REPLICA, PACK, D), 1.0, 6.0, ((0, 2), (2, 8), (3, 8)))
    image_of_token = draw_image_of_token(jax.random.fold_in(splits[14], 71), 0)
    ln1_gain = jnp.clip(1.0 + 0.1 * jax.random.normal(splits[2], (N_SECTION, D), jnp.float32), 0.5, 1.5).astype(jnp.bfloat16)
    ln1_bias = bell_draw(splits[3], (N_SECTION, D), 0.2, 1.25, ((0, 2), (1, 8)))
    w_qkv = bell_draw(splits[4], (N_SECTION, D, 3 * D), D ** -0.5, 0.1875, ((0, 2), (1, 8)))
    qv_bias = bell_draw(splits[5], (N_SECTION, 2 * D), 0.2, 1.25, ((0, 2), (1, 8)))
    w_out = bell_draw(splits[6], (N_SECTION, D, D), (max(D // 256, 1)) ** -0.5, 3.0, ((0, 2), (1, 8)))
    out_bias = bell_draw(splits[7], (N_SECTION, D), 0.2, 1.25, ((0, 2), (1, 8)))
    ln2_gain = jnp.clip(1.0 + 0.1 * jax.random.normal(splits[8], (N_SECTION, D), jnp.float32), 0.5, 1.5).astype(jnp.bfloat16)
    ln2_bias = bell_draw(splits[9], (N_SECTION, D), 0.2, 1.25, ((0, 2), (1, 8)))
    w_fc1 = bell_draw(splits[10], (N_SECTION, D, FF), D ** -0.5, 0.1875, ((0, 2), (1, 8)))
    fc1_bias = bell_draw(splits[11], (N_SECTION, FF), 0.2, 1.25, ((0, 2), (1, 8)))
    w_fc2 = bell_draw(splits[12], (N_SECTION, FF, D), FF ** -0.5, 0.09375, ((0, 2), (1, 8)))
    fc2_bias = bell_draw(splits[13], (N_SECTION, D), 0.2, 1.25, ((0, 2), (1, 8)))
    return {"boundary": boundary, "image_of_token": image_of_token, "ln1_gain": ln1_gain, "ln1_bias": ln1_bias, "w_qkv": w_qkv, "qv_bias": qv_bias, "w_out": w_out, "out_bias": out_bias, "ln2_gain": ln2_gain, "ln2_bias": ln2_bias, "w_fc1": w_fc1, "fc1_bias": fc1_bias, "w_fc2": w_fc2, "fc2_bias": fc2_bias}


@jax.custom_vjp
def low(v):
    return lax.optimization_barrier(v.astype(jnp.bfloat16)).astype(jnp.float32)

@jax.custom_vjp
def low_back(v):
    return v

def low_keep(v):
    return (low(v), None)

def low_pass(kept, grad):
    return (grad,)

def back_keep(v):
    return (v, None)

def back_low(kept, grad):
    return (low(grad),)
low.defvjp(low_keep, low_pass)
low_back.defvjp(back_keep, back_low)
EPS = 1e-06
NEG = -1e+30

def product(first_op, second_op):
    return jnp.dot(first_op, second_op, precision=lax.Precision.HIGHEST, preferred_element_type=jnp.float32)

def layer_norm(resid_in, gain_vec, offset):
    centered = resid_in - lax.optimization_barrier(jnp.mean(resid_in, axis=-1, keepdims=True))
    variance = lax.optimization_barrier(jnp.mean(centered * centered, axis=-1, keepdims=True))
    return centered * lax.rsqrt(variance + EPS) * gain_vec + offset

def block_forward(weights, resid_in, image_ids):
    ln1_gain, ln1_bias, w_qkv, qv_bias, w_out, out_bias, ln2_gain, ln2_bias, w_fc1, fc1_bias, w_fc2, fc2_bias = weights
    token_count = resid_in.shape[0]
    score_scale = 1.0 / math.sqrt(HEAD)
    normed_one = low(layer_norm(resid_in, ln1_gain, ln1_bias))
    bias_full = jnp.concatenate([qv_bias[:D], jnp.zeros_like(qv_bias[:D]), qv_bias[D:]])
    projected = low_back(low(product(normed_one, w_qkv) + bias_full))
    queries = projected[:, :D].reshape(token_count, HEADS, HEAD)
    key_rows = projected[:, D:2 * D].reshape(token_count, HEADS, HEAD)
    value_rows = projected[:, 2 * D:].reshape(token_count, HEADS, HEAD)
    raw_scores = jnp.einsum('qhd,khd->hqk', queries, key_rows, precision=lax.Precision.HIGHEST) * score_scale
    raw_scores = low_back(raw_scores)
    same_image = (image_ids[:, None] == image_ids[None, :])[None]
    scores = jnp.where(same_image, raw_scores, NEG)
    shifted = jnp.exp(scores - lax.optimization_barrier(jnp.max(scores, axis=-1, keepdims=True)))
    attn_probs = shifted / lax.optimization_barrier(jnp.sum(shifted, axis=-1, keepdims=True))
    weighted = jnp.einsum('hqk,khd->qhd', low(attn_probs), value_rows, precision=lax.Precision.HIGHEST)
    weighted = low_back(low(weighted.reshape(token_count, D)))
    resid_mid = resid_in + low_back(product(weighted, w_out) + out_bias)
    normed_two = low(layer_norm(resid_mid, ln2_gain, ln2_bias))
    hidden = low_back(product(normed_two, w_fc1) + fc1_bias)
    activated = low(jax.nn.gelu(hidden, approximate=False))
    return resid_mid + low_back(product(activated, w_fc2) + fc2_bias)

def pack_forward(weights, pack_input, image_ids):
    lower_weights = tuple((member[0] for member in weights))
    upper_weights = tuple((member[1] for member in weights))
    carried = low_back(low(block_forward(lower_weights, pack_input, image_ids)))
    return block_forward(upper_weights, carried, image_ids)

def reference(boundary, image_of_token, ln1_gain, ln1_bias, w_qkv, qv_bias, w_out, out_bias, ln2_gain, ln2_bias, w_fc1, fc1_bias, w_fc2, fc2_bias):
    weights = tuple((member.astype(jnp.float32) for member in (ln1_gain, ln1_bias, w_qkv, qv_bias, w_out, out_bias, ln2_gain, ln2_bias, w_fc1, fc1_bias, w_fc2, fc2_bias)))
    pack_count = MICRO * N_REPLICA
    inputs = boundary[0].astype(jnp.float32).reshape(pack_count, PACK, D)
    cotangent = boundary[1].astype(jnp.float32).reshape(pack_count, PACK, D)
    image_table = image_of_token.reshape(pack_count, PACK)

    def forward_all(weight_set, input_set):

        def one_pack(packed):
            return pack_forward(weight_set, packed[0], packed[1])
        return lax.map(jax.checkpoint(one_pack), (input_set, image_table))
    outputs, pullback = jax.vjp(forward_all, weights, inputs)
    weight_grads, input_grads = pullback(cotangent)
    boundary_out = jnp.stack([input_grads, outputs]).reshape(N_SECTION, MICRO, N_REPLICA, PACK, D)
    return (boundary_out, weight_grads[0], weight_grads[1], weight_grads[2], weight_grads[3], weight_grads[4], weight_grads[5], weight_grads[6], weight_grads[7], weight_grads[8], weight_grads[9], weight_grads[10], weight_grads[11])
```

```python
import functools

import jax
import jax.numpy as jnp
from jax import lax
from jax.experimental import pallas as pl
from jax.experimental.pallas import tpu as pltpu
from jax.sharding import PartitionSpec as P

D = 1024
HEADS = 16
HEAD = 64
FF = 4096
EPS = 1e-06
NEG = -1e30

MICRO = 2
CHIPS = 4
ROWS = 96
TOK = CHIPS * ROWS
KEYS = 2 * TOK
WQ = 3 * D // CHIPS
WO = D // CHIPS
W1 = FF // CHIPS
REPL = 8

MESH = pl.DeviceIdType.MESH
F32 = jnp.float32
BF16 = jnp.bfloat16

AG1, RS1, AG2, RS2, BAG1, BRS1, BAG2, BRS2 = range(8)


def mm(a, b):
    return jnp.dot(a, b, preferred_element_type=F32)


def mm_t(a, b):
    return lax.dot_general(a, b, (((1,), (1,)), ((), ())), preferred_element_type=F32)


def over_rows(a, b):
    return lax.dot_general(a, b, (((0,), (0,)), ((), ())), preferred_element_type=F32)


def norm_parts(v):
    centered = v - jnp.mean(v, axis=-1, keepdims=True)
    rstd = lax.rsqrt(jnp.mean(centered * centered, axis=-1, keepdims=True) + EPS)
    return centered * rstd, rstd


def gray(k):
    return k + k // 2 - 2 * (k // 3)


def flip(r):
    return r + 1 - 2 * lax.rem(r, 2)


def copy_to(src, dst, send, recv, where):
    return pltpu.make_async_remote_copy(
        src_ref=src, dst_ref=dst, send_sem=send, recv_sem=recv, device_id=where, device_id_type=MESH
    )


QKV = {1: 0, 5: 1, 6: 2}


def piece_kinds():
    table = {kind: (0, 1, 3, 2) for kind in (0, 1, 2, 5, 6)}
    table.update({3: (0,), 4: (0,)})
    return table


def step_kernel(
    bnd, idr, v_ln1g, v_ln1b, v_qv, v_out, v_ln2g, v_ln2b, v_fc1, v_fc2, wq_s, wo_s, w1_s, w2_s,
    edge_o, fv, f1, fa, fc, f2,
    idc, vec_s, vecs, wq, wo, w1, w2,
    n1, n2, act, dgl, qkv, kvp, wt, rin, rmid, g, ga, dh, dp, dw,
    stage, landed, swap, carry_s, carry_r, dkv, dkv_s, dkv_r, own, gnext,
    pga, pgb, pgc, pgd, rga, rgb, rgc, rgd, lga, lgb, lgc, lgd,
    vg_o, em, ea, ec, zm, za, zc, ym, ya, yc, pm, p2, pa, pc, q1, qt, qa, lv, tv, zv, yv,
    xs_sem, xr_sem, ks_sem, kr_sem, ds_sem, dr_sem, cs_sem, cr_sem,
    wxs, wxr, wns, wnr, was, war, wfs, wfr, loc_sem, ps_sem, pr_sem, rs_sem, rr_sem, out_sem,
    zs_sem, zr_sem, as_sem, ar_sem, hs_sem, hr_sem, ys_sem, yr_sem, vs_sem, vr_sem, us_sem, ur_sem,
):
    sec = lax.axis_index("section")
    me = lax.axis_index("shard")
    rep = lax.axis_index("replica")
    x = me // 2
    c = me % 2
    mate = {"shard": x * 2 + 1 - c}
    other = {"section": 1 - sec}
    across_to = {"section": 1 - sec, "replica": flip(rep)}
    kinds = piece_kinds()

    def peer(d):
        return lax.rem(x + d, CHIPS)

    def at_peer(d):
        return {"shard": peer(d) * 2 + c}

    def at_rep(j):
        return {"replica": lax.rem(rep + j, REPL)}

    def at_shard(j):
        return {"shard": lax.rem(me + j, 8)}

    barrier = pltpu.get_barrier_semaphore()
    for j in range(1, REPL):
        pl.semaphore_signal(barrier, inc=1, device_id=at_shard(j), device_id_type=MESH)
        pl.semaphore_signal(barrier, inc=1, device_id=at_rep(j), device_id_type=MESH)
    for where in (other, across_to):
        pl.semaphore_signal(barrier, inc=1, device_id=where, device_id_type=MESH)
    pl.semaphore_wait(barrier, 16)

    def rows_of(chip):
        return pl.ds(pl.multiple_of(chip * ROWS, 32), ROWS)

    def w_src(kind, chip):
        if kind == 0:
            return vec_s
        if kind in (1, 5, 6):
            return wq_s.at[:, pl.ds(pl.multiple_of(QKV[kind] * D + chip * WO, WO), WO)]
        if kind == 2:
            return w1_s.at[:, pl.ds(pl.multiple_of(chip * W1, W1), W1)]
        return wo_s if kind == 3 else w2_s

    def w_dst(layer, kind, chip, core):
        if kind == 0:
            return vecs.at[layer, chip * 2 + core]
        if kind in (1, 2, 5, 6):
            rows = pl.ds(pl.multiple_of((chip * 2 + core) * 128, 128), 128)
            if kind == 2:
                return w1.at[layer, rows]
            return wq.at[layer, rows, pl.ds(QKV[kind] * WO, WO)]
        if kind == 3:
            return wo.at[layer, pl.ds(pl.multiple_of(core * 128, 128), 128)]
        return w2.at[layer, pl.ds(pl.multiple_of(core * 512, 512), 512)]

    def x_copy(kind, d, owner):
        return copy_to(
            w_src(kind, peer(d)), w_dst(sec, kind, owner, c), wxs.at[kind, d], wxr.at[kind, d], at_peer(d)
        )

    def own_piece(kind, d):
        return w_src(kind, x) if d == 0 else w_dst(sec, kind, peer(4 - d), c)

    def near_copy(kind, d, core):
        dst = w_dst(sec, kind, peer(4 - d), core)
        return copy_to(own_piece(kind, d), dst, wns.at[kind, d], wnr.at[kind, d], mate)

    def across_copy(kind, d, layer):
        dst = w_dst(layer, kind, peer(4 - d), c)
        return copy_to(own_piece(kind, d), dst, was.at[kind, d], war.at[kind, d], across_to)

    def far_copy(kind, d, core):
        ref = w_dst(1 - sec, kind, peer(4 - d), core)
        return copy_to(ref, ref, wfs.at[kind, d], wfr.at[kind, d], mate)

    def local_copy(kind):
        return pltpu.make_async_copy(w_src(kind, x), w_dst(sec, kind, x, c), loc_sem.at[kind])

    def launch(kind):
        if kind not in (3, 4):
            for d in (1, 3, 2):
                x_copy(kind, d, x).start()
        near_copy(kind, 0, c).start()
        local_copy(kind).start()

    def settle_near(kind):
        across_copy(kind, 0, sec).start()
        for d in kinds[kind][1:]:
            x_copy(kind, d, peer(4 - d)).wait_recv()
            near_copy(kind, d, c).start()
            across_copy(kind, d, sec).start()
        local_copy(kind).wait()
        for d in kinds[kind]:
            near_copy(kind, d, 1 - c).wait_recv()

    def settle_far(kind):
        for d in kinds[kind]:
            across_copy(kind, d, 1 - sec).wait_recv()
            far_copy(kind, d, c).start()
        for d in kinds[kind]:
            far_copy(kind, d, 1 - c).wait_recv()

    swap_copy = copy_to(bnd.at[1 - sec], swap, cs_sem.at[0], cr_sem.at[0], other)
    carry_copy = copy_to(carry_s, carry_r, cs_sem.at[1], cr_sem.at[1], other)

    at = 0
    for v in (v_ln1g, v_ln1b, v_qv, v_out, v_ln2g, v_ln2b, v_fc1, v_fc2):
        for t in range(v.shape[1] // 128):
            vec_s[at : at + 1, :] = v[:, t * 128 : t * 128 + 128].astype(F32)
            at += 1
    launch(0)
    swap_copy.start()
    for kind in QKV:
        launch(kind)
    idc[...] = jnp.transpose(jnp.broadcast_to(idr[:1, :], (128, KEYS)))
    settle_near(0)
    settle_far(0)
    swap_copy.wait_recv()

    @pl.when(sec == 0)
    def _():
        rin[0] = bnd[0].astype(F32)
        gnext[...] = swap[...].astype(F32)

    @pl.when(sec == 1)
    def _():
        rin[0] = swap[...].astype(F32)
        gnext[...] = bnd[1].astype(F32)

    def vec_row(l, k):
        return jnp.concatenate([vecs[l, i, k : k + 1, :] for i in range(8)], axis=1)

    def pieces(l, i, ks):
        part = vecs[l, i]
        return [part[k : k + 1, :] for k in ks]

    def gather_copy(buf, kind, l, d, owner):
        ref = buf.at[l, rows_of(owner)]
        return copy_to(ref, ref, xs_sem.at[kind, l, d], xr_sem.at[kind, l, d], at_peer(d))

    def scatter_copy(kind, l, d):
        return copy_to(
            stage.at[d - 1],
            landed.at[kind // 2, d - 1],
            xs_sem.at[kind, l, d],
            xr_sem.at[kind, l, d],
            at_peer(d),
        )

    def gather_start(buf, kind, l):
        for d in (1, 3, 2):
            gather_copy(buf, kind, l, d, x).start()

    def gather_wait(buf, kind, l, d):
        gather_copy(buf, kind, l, d, peer(4 - d)).wait_recv()

    def scatter_add(kind, l, base):
        total = base
        for d in (1, 3, 2):
            scatter_copy(kind, l, d).wait_recv()
            total = total + landed[kind // 2, d - 1].astype(F32)
        for d in (1, 3, 2):
            scatter_copy(kind, l, d).wait_send()
        return total

    def send_part(kind, l, d, part):
        @pl.when(d == 0)
        def _():
            own[...] = part

        @pl.when(d != 0)
        def _():
            stage[d - 1] = part.astype(BF16)
            scatter_copy(kind, l, d).start()

    def kv_copy(l, d):
        rows = rows_of(peer(4 - d))
        return copy_to(
            qkv.at[l, rows, pl.ds(WO, 2 * WO)], kvp.at[l, rows], ks_sem.at[l, d], kr_sem.at[l, d], mate
        )

    lane = lax.broadcasted_iota(jnp.int32, (1, 128), 1)

    def forward(l, first):
        need_far = l + sec == 1
        qkv_b = jnp.concatenate(
            pieces(l, x, (2, 3)) + [jnp.zeros((1, WO), F32)] + pieces(l, 4 + x, (2, 3)), axis=1
        )
        fc1_b = jnp.concatenate(
            pieces(l, 2 * x, (7, 8, 9, 10)) + pieces(l, 2 * x + 1, (7, 8, 9, 10)), axis=1
        )
        normed, _ = norm_parts(rin[l])
        n1[l, rows_of(x)] = (normed * vec_row(l, 0) + vec_row(l, 1)).astype(BF16)
        gather_start(n1, AG1, l)

        @pl.when(l == 0)
        def _():
            for kind in QKV:
                settle_near(kind)
            launch(3)
            launch(2)
            launch(4)

        @pl.when(need_far)
        def _():
            for kind in QKV:
                settle_far(kind)

        def project(k, _):
            d = gray(k)
            rows = rows_of(peer(4 - d))

            @pl.when(d != 0)
            def _():
                gather_wait(n1, AG1, l, d)

            qkv[l, rows] = (mm(n1[l, rows], wq[l]) + qkv_b).astype(BF16)
            kv_copy(l, d).start()
            return 0

        lax.fori_loop(0, CHIPS, project, 0)

        @pl.when(l == 0)
        def _():
            settle_near(3)
            settle_near(2)

        @pl.when(need_far)
        def _():
            settle_far(3)

        for d in range(CHIPS):
            kv_copy(l, d).wait_recv()

        def attend(j, _):
            d = gray(lax.rem(j + 1, CHIPS))
            rows = rows_of(peer(d))
            bias = jnp.where(idc[rows][:, :1] == idr[:1, :], 0.0, NEG)
            for pair in range(2):
                lanes = slice(pair * 128, pair * 128 + 128)
                q = qkv[l, rows, lanes] * jnp.asarray(HEAD**-0.5, BF16)
                k_own = qkv[l, :, WO + pair * 128 : WO + pair * 128 + 128]
                v_own = qkv[l, :, 2 * WO + pair * 128 : 2 * WO + pair * 128 + 128]
                k_par = kvp[l, :, lanes]
                v_par = kvp[l, :, WO + pair * 128 : WO + pair * 128 + 128]
                outs = []
                for half in range(2):
                    qm = jnp.where(lane // HEAD == half, q, jnp.zeros_like(q))
                    s = jnp.concatenate([mm_t(qm, k_own), mm_t(qm, k_par)], axis=1) + bias
                    p = jnp.exp(s - jnp.max(s, axis=1, keepdims=True))
                    p = (p / jnp.sum(p, axis=1, keepdims=True)).astype(BF16)
                    outs.append(mm(p[:, :TOK], v_own) + mm(p[:, TOK:], v_par))
                wt[l, rows, lanes] = jnp.where(lane < HEAD, outs[0], outs[1]).astype(BF16)
            send_part(RS1, l, d, mm(wt[l, rows], wo[l]))
            return 0

        lax.fori_loop(0, CHIPS, attend, 0)
        rmid[l] = rin[l] + (scatter_add(RS1, l, own[...]) + vec_row(l, 4))
        normed, _ = norm_parts(rmid[l])
        n2[l, rows_of(x)] = (normed * vec_row(l, 5) + vec_row(l, 6)).astype(BF16)
        gather_start(n2, AG2, l)

        @pl.when(l == 0)
        def _():
            settle_near(4)

        @pl.when(need_far)
        def _():
            settle_far(2)
            settle_far(4)

        def feed(k, _):
            d = gray(k)
            back = lax.rem(4 - d, CHIPS)
            rows = rows_of(peer(back))

            @pl.when(d != 0)
            def _():
                gather_wait(n2, AG2, l, d)

            h = mm(n2[l, rows], w1[l]) + fc1_b
            phi = 0.5 + 0.5 * lax.erf(h * (0.5**0.5))
            act[l, rows] = (h * phi).astype(BF16)
            dgl[l, rows] = phi + h * (jnp.exp(-0.5 * h * h) * 0.3989422804014327)
            send_part(RS2, l, back, mm(act[l, rows], w2[l]))
            return 0

        lax.fori_loop(0, CHIPS, feed, 0)
        out = rmid[l] + (scatter_add(RS2, l, own[...]) + vec_row(l, 11))

        @pl.when(l == 0)
        def _():
            rin[1] = out.astype(BF16).astype(F32)

        @pl.when((l == 1) & (sec == 0))
        def _():
            carry_s[...] = out.astype(BF16)
            carry_copy.start()

        @pl.when((l == 1) & (sec == 1))
        def _():
            edge_o[1] = out

        return first

    lax.fori_loop(0, 2, forward, 0)

    vg_o[...] = jnp.zeros_like(vg_o)

    def col_sum(v):
        return jnp.sum(v, axis=0, keepdims=True)

    def dkv_copy(l):
        return copy_to(dkv_s.at[l], dkv_r.at[l], ds_sem.at[l], dr_sem.at[l], mate)

    def grads_mlp(l):
        def block(t, _):
            cols = pl.ds(pl.multiple_of(t * 256, 256), 256)
            pgb[t] = over_rows(n2[l, :, cols], dh[l]).astype(BF16).reshape(2, 128, W1)
            half = pl.ds(pl.multiple_of(lax.rem(t, 2) * 256, 256), 256)
            pgd[t // 2, half] = over_rows(act[l, :, cols], g[l]).astype(BF16)
            return 0

        lax.fori_loop(0, CHIPS, block, 0)

    def grads_att(l):
        def block(t, _):
            cols = pl.ds(pl.multiple_of(t * 256, 256), 256)
            pga[t] = over_rows(n1[l, :, cols], dp[l]).astype(BF16).reshape(2, 128, WQ)
            return 0

        lax.fori_loop(0, CHIPS, block, 0)
        pgc[...] = over_rows(wt[l], ga[l]).astype(BF16).reshape(2, 128, D)

    def pair_mlp(l):
        return (
            copy_to(pgb.at[:, 1 - c], rgb, ps_sem.at[l, 1], pr_sem.at[l, 1], mate),
            copy_to(pgd.at[1 - c], rgd, ps_sem.at[l, 3], pr_sem.at[l, 3], mate),
        )

    def pair_att(l):
        return (
            copy_to(pga.at[:, 1 - c], rga, ps_sem.at[l, 0], pr_sem.at[l, 0], mate),
            copy_to(pgc.at[1 - c], rgc, ps_sem.at[l, 2], pr_sem.at[l, 2], mate),
        )

    def piece_of(l, r):
        return r + (l + sec - 2 * l * sec) * (1 - 2 * lax.rem(r, 2))

    def few(p):
        return pl.ds(pl.multiple_of(p * 16, 16), 16)

    def more(p):
        return pl.ds(pl.multiple_of(p * 64, 64), 64)

    def spread_copy(l, n, j):
        p = piece_of(l, lax.rem(rep + j, REPL))
        src = (rga.at[:, few(p)], rgb.at[:, few(p)], rgc.at[few(p)], rgd.at[more(p)])[n]
        return copy_to(src, (lga, lgb, lgc, lgd)[n].at[l, j], rs_sem.at[l, n, j], rr_sem.at[l, n, j], at_rep(j))

    def each_piece(l, ns, act_on):
        def one(j, _):
            for n in ns:
                act_on(spread_copy(l, n, j))
            return 0

        lax.fori_loop(1, REPL, one, 0)

    def sent(cp):
        cp.wait_send()

    def arrived(cp):
        cp.wait_recv()

    def begin(cp):
        cp.start()

    def both(u, v):
        return (u.astype(F32) + v.astype(F32)).astype(BF16)

    def spread_mlp(l):
        for cp in pair_mlp(l):
            cp.wait_recv()
        for t in range(CHIPS):
            rgb[t] = both(pgb[t, c], rgb[t])
        rgd[...] = both(pgd[c], rgd[...])
        p = piece_of(l, rep)
        for t in range(CHIPS):
            em[l, t * 16 : t * 16 + 16] = rgb[t, few(p)].astype(F32)
        em[l, 64:] = rgd[more(p)].astype(F32)
        each_piece(l, (1, 3), begin)

    def spread_att(l):
        for cp in pair_att(l):
            cp.wait_recv()
        for t in range(CHIPS):
            rga[t] = both(pga[t, c], rga[t])
        rgc[...] = both(pgc[c], rgc[...])
        p = piece_of(l, rep)
        for t in range(CHIPS):
            ea[l, t * 16 : t * 16 + 16] = rga[t, few(p)].astype(F32)
        ec[l] = rgc[few(p)].astype(F32)
        each_piece(l, (0, 2), begin)

    def collect_mlp(l):
        each_piece(l, (1, 3), arrived)
        for t in range(CHIPS):
            rows = slice(t * 16, t * 16 + 16)
            total = em[l, rows]
            for j in range(1, REPL):
                total = total + lgb[l, j, t].astype(F32)
            em[l, rows] = total
        total = em[l, 64:]
        for j in range(1, REPL):
            total = total + lgd[l, j].astype(F32)
        em[l, 64:] = total

    def collect_att(l):
        each_piece(l, (0, 2), arrived)
        for t in range(CHIPS):
            rows = slice(t * 16, t * 16 + 16)
            total = ea[l, rows]
            for j in range(1, REPL):
                total = total + lga[l, j, t].astype(F32)
            ea[l, rows] = total
        total = ec[l]
        for j in range(1, REPL):
            total = total + lgc[l, j].astype(F32)
        ec[l] = total

    def backward(i, first):
        l = 1 - i

        def add_vec(k, v):
            vg_o[l, k : k + 1, : v.shape[1]] += v

        def norm_back(v, gain, dy, k):
            xhat, rstd = norm_parts(v)
            add_vec(k, col_sum(dy * xhat))
            add_vec(k + 1, col_sum(dy))
            dyg = dy * gain
            return rstd * (
                dyg - jnp.mean(dyg, axis=-1, keepdims=True) - xhat * jnp.mean(dyg * xhat, axis=-1, keepdims=True)
            )

        low = gnext[...].astype(BF16)
        g[l, rows_of(x)] = low
        gather_start(g, BAG1, l)
        add_vec(7, col_sum(low.astype(F32)))

        @pl.when(i == 1)
        def _():
            grads_att(1)
            each_piece(1, (1, 3), sent)
            for cp in pair_att(1):
                cp.start()
            collect_mlp(1)

        def feed(k, _):
            d = gray(k)
            back = lax.rem(4 - d, CHIPS)
            rows = rows_of(peer(back))

            @pl.when(d != 0)
            def _():
                gather_wait(g, BAG1, l, d)

            d_low = (mm_t(g[l, rows], w2[l]) * dgl[l, rows]).astype(BF16)
            dh[l, rows] = d_low
            add_vec(6, col_sum(d_low.astype(F32)))
            send_part(BRS1, l, back, mm_t(d_low, w1[l]))
            return 0

        lax.fori_loop(0, CHIPS, feed, 0)

        @pl.when(i == 1)
        def _():
            spread_att(1)
            for cp in pair_mlp(1):
                cp.wait_send()

        grads_mlp(l)
        for cp in pair_mlp(l):
            cp.start()
        dn2 = scatter_add(BRS1, l, own[...])
        d_mid = gnext[...] + norm_back(rmid[l], vec_row(l, 5), dn2, 4)
        rmid[l] = d_mid
        low = d_mid.astype(BF16)
        ga[l, rows_of(x)] = low
        gather_start(ga, BAG2, l)
        add_vec(3, col_sum(low.astype(F32)))

        def expand(k, _):
            d = gray(k)
            rows = rows_of(peer(4 - d))

            @pl.when(d != 0)
            def _():
                gather_wait(ga, BAG2, l, d)

            dw[rows] = mm_t(ga[l, rows], wo[l]).astype(BF16)
            return 0

        lax.fori_loop(0, CHIPS, expand, 0)
        spread_mlp(l)
        dkv[...] = jnp.zeros_like(dkv)

        def attend(b, _):
            rows = pl.ds(pl.multiple_of(b * 128, 128), 128)
            bias = jnp.where(idc[:, :1] == idr[:, rows][:1, :], 0.0, NEG)
            for pair in range(2):
                lanes = slice(pair * 128, pair * 128 + 128)
                q = qkv[l, rows, lanes] * jnp.asarray(HEAD**-0.5, BF16)
                do = dw[rows, lanes]
                k_all = jnp.concatenate(
                    [qkv[l, :, WO + pair * 128 : WO + pair * 128 + 128], kvp[l, :, lanes]], axis=0
                )
                v_all = jnp.concatenate(
                    [
                        qkv[l, :, 2 * WO + pair * 128 : 2 * WO + pair * 128 + 128],
                        kvp[l, :, WO + pair * 128 : WO + pair * 128 + 128],
                    ],
                    axis=0,
                )
                dqs = []
                for half in range(2):
                    keep = lane // HEAD == half
                    qm = jnp.where(keep, q, jnp.zeros_like(q))
                    dom = jnp.where(keep, do, jnp.zeros_like(do))
                    s = mm_t(k_all, qm) + bias
                    p = jnp.exp(s - jnp.max(s, axis=0, keepdims=True))
                    p = p * (1.0 / jnp.sum(p, axis=0, keepdims=True))
                    dpr = mm_t(v_all, dom)
                    ds = (p * (dpr - jnp.sum(p * dpr, axis=0, keepdims=True))).astype(BF16)
                    dkv[:, lanes] += mm(ds, qm)
                    dkv[:, WO + pair * 128 : WO + pair * 128 + 128] += mm(p.astype(BF16), dom)
                    dqs.append(over_rows(ds, k_all))
                dq = jnp.where(lane < HEAD, dqs[0], dqs[1]) * (HEAD**-0.5)
                dp[l, rows, lanes] = dq.astype(BF16)
            return 0

        lax.fori_loop(0, TOK // 128, attend, 0)
        dkv_s[l] = dkv[TOK:].astype(BF16)

        @pl.when(i == 1)
        def _():
            collect_att(1)
            each_piece(1, (0, 2), sent)

        dkv_copy(l).start()
        dkv_copy(l).wait_recv()
        dp[l, :, WO:] = (dkv[:TOK] + dkv_r[l].astype(F32)).astype(BF16)
        add_vec(
            2,
            jnp.concatenate(
                [col_sum(dp[l, :, :WO].astype(F32)), col_sum(dp[l, :, 2 * WO :].astype(F32))], axis=1
            ),
        )

        @pl.when(i == 1)
        def _():
            for cp in pair_att(1):
                cp.wait_send()
            grads_att(0)
            for cp in pair_att(0):
                cp.start()

        def shrink(j, _):
            d = gray(lax.rem(j + 1, CHIPS))
            send_part(BRS2, l, d, mm_t(dp[l, rows_of(peer(d))], wq[l]))
            return 0

        lax.fori_loop(0, CHIPS, shrink, 0)

        @pl.when(i == 1)
        def _():
            spread_att(0)

        dn1 = scatter_add(BRS2, l, own[...])
        d_in = rmid[l] + norm_back(rin[l], vec_row(l, 0), dn1, 0)

        @pl.when(i == 0)
        def _():
            gnext[...] = d_in.astype(BF16).astype(F32)

        @pl.when((i == 1) & (sec == 1))
        def _():
            carry_s[...] = d_in.astype(BF16)
            carry_copy.start()

        @pl.when((i == 1) & (sec == 0))
        def _():
            edge_o[0] = d_in

        return first

    lax.fori_loop(0, 2, backward, 0)

    def vec_copy(j):
        return copy_to(vg_o, lv.at[j], vs_sem.at[j], vr_sem.at[j], at_rep(j))

    def vec_share(j, slot):
        return copy_to(tv, fv.at[slot], us_sem.at[j], ur_sem.at[j], at_shard(j))

    def cross_copy(n):
        src, dst = ((zm, ym), (za, ya), (zc, yc), (zv, yv))[n]
        return copy_to(src, dst, zs_sem.at[n], zr_sem.at[n], across_to)

    def turn_refs(n, source):
        if n == 0:
            return pm, q1.at[:, pl.ds(pl.multiple_of(source * W1, W1), W1)]
        return pa, qt.at[few(source)]

    def turn_copy(n, d, source):
        src, dst = turn_refs(n, source)
        return copy_to(src.at[few(peer(d))], dst, as_sem.at[n, d], ar_sem.at[n, d], at_peer(d))

    def turn_start(n):
        for d in (1, 3, 2):
            turn_copy(n, d, x).start()
        src, dst = turn_refs(n, x)
        dst[...] = src[few(x)]

    def turn_wait(n):
        for d in (1, 3, 2):
            turn_copy(n, d, peer(4 - d)).wait_recv()

    zi = rep // 2
    yi = lax.rem(rep, 2)
    y_mate = {"replica": flip(rep)}
    pieces_of = ((q1, f1), (qa, fa), (pc, fc), (p2, f2))

    def slot_ref(n, slot):
        return pieces_of[n][1].at[more(slot) if n == 3 else few(slot)]

    def slot_of(d, y):
        return lax.rem(zi + 4 - d, 4) * 2 + y

    def along_z(n, d, slot):
        src = pieces_of[n][0]
        where = {"replica": lax.rem(zi + d, 4) * 2 + yi}
        return copy_to(src, slot_ref(n, slot), hs_sem.at[n, d], hr_sem.at[n, d], where)

    def along_y(n, d, y):
        dst = slot_ref(n, slot_of(d, y))
        return copy_to(pieces_of[n][0] if d == 0 else dst, dst, ys_sem.at[n, d], yr_sem.at[n, d], y_mate)

    def keep_piece(n):
        return pltpu.make_async_copy(pieces_of[n][0], slot_ref(n, rep), out_sem.at[n])

    def share_start(n):
        along_y(n, 0, yi).start()
        for d in (1, 3, 2):
            along_z(n, d, rep).start()
        keep_piece(n).start()

    def share_on(n):
        for d in (1, 3, 2):
            along_z(n, d, slot_of(d, yi)).wait_recv()
            along_y(n, d, yi).start()

    for j in range(1, REPL):
        vec_copy(j).start()
    collect_mlp(0)
    zm[...] = em[1 - sec].astype(BF16)
    cross_copy(0).start()
    total = vg_o[...]
    for j in range(1, REPL):
        vec_copy(j).wait_recv()
        total = total + lv[j]
    vg_o_sum = total
    zv[...] = jnp.where(sec == 0, vg_o_sum[1], vg_o_sum[0])
    cross_copy(3).start()
    cross_copy(0).wait_recv()
    pm[...] = (em[sec, :64] + ym[:64].astype(F32)).astype(BF16)
    p2[...] = (em[sec, 64:] + ym[64:].astype(F32)).astype(BF16)
    turn_start(0)
    share_start(3)
    turn_wait(0)
    share_start(0)
    collect_att(0)
    za[...] = ea[1 - sec].astype(BF16)
    zc[...] = ec[1 - sec].astype(BF16)
    cross_copy(1).start()
    cross_copy(2).start()
    cross_copy(3).wait_recv()
    tv[...] = jnp.where(sec == 0, vg_o_sum[0], vg_o_sum[1]) + yv[...]
    fv[me] = tv[...]
    for j in range(1, REPL):
        vec_share(j, me).start()
    cross_copy(1).wait_recv()
    cross_copy(2).wait_recv()
    pa[...] = (ea[sec] + ya[...].astype(F32)).astype(BF16)
    pc[...] = (ec[sec] + yc[...].astype(F32)).astype(BF16)
    turn_start(1)
    share_start(2)
    turn_wait(1)
    for t in range(3):
        for chip in range(CHIPS):
            at = t * D + chip * WO
            qa[:, at : at + WO] = qt[chip * 16 : chip * 16 + 16, t * WO : t * WO + WO]
    share_start(1)
    share_on(3)
    share_on(0)
    share_on(2)
    share_on(1)
    for n in range(4):
        for d in range(4):
            along_y(n, d, 1 - yi).wait_recv()
        keep_piece(n).wait()
    for j in range(1, REPL):
        vec_share(j, lax.rem(me + 8 - j, 8)).wait_recv()

    carry_copy.wait_recv()
    edge_o[1 - sec] = carry_r[...].astype(F32)
    carry_copy.wait_send()
    swap_copy.wait_send()
    for kind in kinds:
        for d in kinds[kind]:
            if d != 0:
                x_copy(kind, d, x).wait_send()
            near_copy(kind, d, c).wait_send()
            across_copy(kind, d, sec).wait_send()
            far_copy(kind, d, c).wait_send()
    for l in range(2):
        for d in (1, 2, 3):
            for buf, kind in ((n1, AG1), (n2, AG2), (g, BAG1), (ga, BAG2)):
                gather_copy(buf, kind, l, d, x).wait_send()
        for d in range(CHIPS):
            kv_copy(l, d).wait_send()
        dkv_copy(l).wait_send()
    each_piece(0, (0, 1, 2, 3), sent)
    for cp in pair_mlp(0) + pair_att(0):
        cp.wait_send()
    for n in range(4):
        cross_copy(n).wait_send()
    for n in range(2):
        for d in (1, 2, 3):
            turn_copy(n, d, x).wait_send()
    for n in range(4):
        for d in (1, 2, 3):
            along_z(n, d, rep).wait_send()
        for d in range(4):
            along_y(n, d, yi).wait_send()
    for j in range(1, REPL):
        vec_copy(j).wait_send()
        vec_share(j, me).wait_send()


def run_step(*operands):
    vm = pl.BlockSpec(memory_space=pltpu.VMEM)
    hbm = pl.BlockSpec(memory_space=pl.ANY)
    sds = jax.ShapeDtypeStruct
    dma = pltpu.SemaphoreType.DMA
    return pl.pallas_call(
        step_kernel,
        out_shape=(
            sds((MICRO, ROWS, D), F32),
            sds((8, 8, D), F32),
            sds((128, FF), BF16),
            sds((128, 3 * D), BF16),
            sds((128, D), BF16),
            sds((512, D), BF16),
        ),
        in_specs=[vm] * 10 + [hbm] * 4,
        out_specs=(vm, vm, hbm, hbm, hbm, hbm),
        scratch_shapes=[
            pltpu.VMEM((KEYS, 128), jnp.int32),
            pltpu.VMEM((16, 128), F32),
            pltpu.VMEM((2, 8, 16, 128), F32),
            pltpu.VMEM((2, D, WQ), BF16),
            pltpu.VMEM((2, WO, D), BF16),
            pltpu.VMEM((2, D, W1), BF16),
            pltpu.VMEM((2, W1, D), BF16),
            pltpu.VMEM((2, TOK, D), BF16),
            pltpu.VMEM((2, TOK, D), BF16),
            pltpu.VMEM((2, TOK, W1), BF16),
            pltpu.VMEM((2, TOK, W1), F32),
            pltpu.VMEM((2, TOK, WQ), BF16),
            pltpu.VMEM((2, TOK, 2 * WO), BF16),
            pltpu.VMEM((2, TOK, WO), BF16),
            pltpu.VMEM((2, ROWS, D), F32),
            pltpu.VMEM((2, ROWS, D), F32),
            pltpu.VMEM((2, TOK, D), BF16),
            pltpu.VMEM((2, TOK, D), BF16),
            pltpu.VMEM((2, TOK, W1), BF16),
            pltpu.VMEM((2, TOK, WQ), BF16),
            pltpu.VMEM((TOK, WO), BF16),
            pltpu.VMEM((3, ROWS, D), BF16),
            pltpu.VMEM((4, 3, ROWS, D), BF16),
            pltpu.VMEM((ROWS, D), BF16),
            pltpu.VMEM((ROWS, D), BF16),
            pltpu.VMEM((ROWS, D), BF16),
            pltpu.VMEM((KEYS, 2 * WO), F32),
            pltpu.VMEM((2, TOK, 2 * WO), BF16),
            pltpu.VMEM((2, TOK, 2 * WO), BF16),
            pltpu.VMEM((ROWS, D), F32),
            pltpu.VMEM((ROWS, D), F32),
            pltpu.VMEM((CHIPS, 2, 128, WQ), BF16),
            pltpu.VMEM((CHIPS, 2, 128, W1), BF16),
            pltpu.VMEM((2, 128, D), BF16),
            pltpu.VMEM((2, 512, D), BF16),
            pltpu.VMEM((CHIPS, 128, WQ), BF16),
            pltpu.VMEM((CHIPS, 128, W1), BF16),
            pltpu.VMEM((128, D), BF16),
            pltpu.VMEM((512, D), BF16),
            pltpu.VMEM((2, REPL, CHIPS, 16, WQ), BF16),
            pltpu.VMEM((2, REPL, CHIPS, 16, W1), BF16),
            pltpu.VMEM((2, REPL, 16, D), BF16),
            pltpu.VMEM((2, REPL, 64, D), BF16),
            pltpu.VMEM((2, 8, D), F32),
            pltpu.VMEM((2, 128, D), F32),
            pltpu.VMEM((2, 64, WQ), F32),
            pltpu.VMEM((2, 16, D), F32),
            pltpu.VMEM((128, D), BF16),
            pltpu.VMEM((64, WQ), BF16),
            pltpu.VMEM((16, D), BF16),
            pltpu.VMEM((128, D), BF16),
            pltpu.VMEM((64, WQ), BF16),
            pltpu.VMEM((16, D), BF16),
            pltpu.VMEM((64, D), BF16),
            pltpu.VMEM((64, D), BF16),
            pltpu.VMEM((64, WQ), BF16),
            pltpu.VMEM((16, D), BF16),
            pltpu.VMEM((16, FF), BF16),
            pltpu.VMEM((64, WQ), BF16),
            pltpu.VMEM((16, 3 * D), BF16),
            pltpu.VMEM((REPL, 2, 8, D), F32),
            pltpu.VMEM((8, D), F32),
            pltpu.VMEM((8, D), F32),
            pltpu.VMEM((8, D), F32),
            dma((8, 2, CHIPS)),
            dma((8, 2, CHIPS)),
            dma((2, CHIPS)),
            dma((2, CHIPS)),
            dma((2,)),
            dma((2,)),
            dma((2,)),
            dma((2,)),
            dma((7, CHIPS)),
            dma((7, CHIPS)),
            dma((7, CHIPS)),
            dma((7, CHIPS)),
            dma((7, CHIPS)),
            dma((7, CHIPS)),
            dma((7, CHIPS)),
            dma((7, CHIPS)),
            dma((7,)),
            dma((2, 4)),
            dma((2, 4)),
            dma((2, 4, REPL)),
            dma((2, 4, REPL)),
            dma((4,)),
            dma((4,)),
            dma((4,)),
            dma((2, CHIPS)),
            dma((2, CHIPS)),
            dma((4, 4)),
            dma((4, 4)),
            dma((4, 4)),
            dma((4, 4)),
            dma((REPL,)),
            dma((REPL,)),
            dma((REPL,)),
            dma((REPL,)),
        ],
        compiler_params=pltpu.CompilerParams(
            collective_id=0, has_side_effects=True, vmem_limit_bytes=62 * 1024 * 1024
        ),
    )(*operands)


def body(
    boundary, image_of_token, ln1_gain, ln1_bias, w_qkv, qv_bias, w_out, out_bias,
    ln2_gain, ln2_bias, w_fc1, fc1_bias, w_fc2, fc2_bias,
):
    me = lax.axis_index("shard")
    x, c = me // 2, me % 2
    sec = lax.axis_index("section")
    bnd = boundary[0, :, 0]
    ids = lax.dynamic_index_in_dim(image_of_token[:, 0], sec, 0, keepdims=False).reshape(CHIPS, 2, ROWS)
    flipped = jnp.where(c == 0, ids, ids[:, ::-1])
    ids = jnp.swapaxes(flipped, 0, 1).reshape(KEYS)
    idr = jnp.broadcast_to(ids[None, :], (8, KEYS))
    edge, fv, f1, fa, fc, f2 = run_step(
        bnd, idr, ln1_gain, ln1_bias, qv_bias, out_bias, ln2_gain, ln2_bias, fc1_bias, fc2_bias,
        w_qkv[0], w_out[0], w_fc1[0], w_fc2[0],
    )
    g_qkv, g_fc1, g_out, g_fc2 = (v.astype(F32) for v in (fa, f1, fc, f2))

    whole = jnp.sum(fv, axis=0)
    pairs = jnp.sum(fv.reshape(CHIPS, 2, 8, D), axis=1)
    wide = jnp.concatenate(
        [whole[k] for k in (0, 1, 3, 4, 5, 7)]
        + [pairs[:, 2, :WO].reshape(-1), pairs[:, 2, WO : 2 * WO].reshape(-1), pairs[:, 6].reshape(-1)]
    )

    def part(at, size):
        return lax.dynamic_slice_in_dim(wide, at + me * size, size)[None]

    return (
        edge[None, :, None],
        part(0, 128),
        part(1024, 128),
        g_qkv[None],
        part(6 * D, 256),
        g_out[None],
        part(2 * D, 128),
        part(3 * D, 128),
        part(4 * D, 128),
        g_fc1[None],
        part(8 * D, 512),
        g_fc2[None],
        part(5 * D, 128),
    )


def solution(mesh):
    row = P("section", "shard")
    mat = P("section", "shard", None)
    edge = P("section", None, "replica", "shard", None)
    in_specs = (edge, P(None, "replica", None), row, row, mat, row, mat, row, row, row, mat, row, mat, row)
    out_specs = (edge, row, row, mat, row, mat, row, row, row, mat, row, mat, row)
    return jax.shard_map(body, mesh=mesh, in_specs=in_specs, out_specs=out_specs, check_vma=False)
```

```python
import functools

import jax
import jax.numpy as jnp
from jax import lax
from jax.experimental import pallas as pl
from jax.experimental.pallas import tpu as pltpu
from jax.sharding import PartitionSpec as P

D = 1024
HEADS = 16
HEAD = 64
FF = 4096
EPS = 1e-06
NEG = -1e30

MICRO = 2
CHIPS = 4
ROWS = 96
TOK = CHIPS * ROWS
KEYS = 2 * TOK
WQ = 3 * D // CHIPS
WO = D // CHIPS
W1 = FF // CHIPS
REPL = 8

MESH = pl.DeviceIdType.MESH
F32 = jnp.float32
BF16 = jnp.bfloat16

AG1, RS1, AG2, RS2, BAG1, BRS1, BAG2, BRS2 = range(8)


def mm(a, b):
    return jnp.dot(a, b, preferred_element_type=F32)


def mm_t(a, b):
    return lax.dot_general(a, b, (((1,), (1,)), ((), ())), preferred_element_type=F32)


def over_rows(a, b):
    return lax.dot_general(a, b, (((0,), (0,)), ((), ())), preferred_element_type=F32)


def norm_parts(v):
    centered = v - jnp.mean(v, axis=-1, keepdims=True)
    rstd = lax.rsqrt(jnp.mean(centered * centered, axis=-1, keepdims=True) + EPS)
    return centered * rstd, rstd


def gray(k):
    return k + k // 2 - 2 * (k // 3)


def flip(r):
    return r + 1 - 2 * lax.rem(r, 2)


def copy_to(src, dst, send, recv, where):
    return pltpu.make_async_remote_copy(
        src_ref=src, dst_ref=dst, send_sem=send, recv_sem=recv, device_id=where, device_id_type=MESH
    )


QKV = {1: 0, 5: 1, 6: 2}


def piece_kinds():
    table = {kind: (0, 1, 3, 2) for kind in (0, 1, 2, 5, 6)}
    table.update({3: (0,), 4: (0,)})
    return table


def step_kernel(
    bnd, idr, v_ln1g, v_ln1b, v_qv, v_out, v_ln2g, v_ln2b, v_fc1, v_fc2, wq_s, wo_s, w1_s, w2_s,
    edge_o, fv, f1, fa, fc, f2,
    idc, vec_s, vecs, wq, wo, w1, w2,
    n1, n2, act, dgl, qkv, kvp, wt, rin, rmid, g, ga, dh, dp, dw,
    stage, landed, swap, carry_s, carry_r, dkv, dkv_s, dkv_r, own, gnext,
    pga, pgb, pgc, pgd, rga, rgb, rgc, rgd, lga, lgb, lgc, lgd,
    vg_o, em, ea, ec, zm, za, zc, ym, ya, yc, pm, p2, pa, pc, q1, qt, qa, lv, tv, zv, yv,
    xs_sem, xr_sem, ks_sem, kr_sem, ds_sem, dr_sem, cs_sem, cr_sem,
    wxs, wxr, wns, wnr, was, war, wfs, wfr, wys, wyr, loc_sem, ps_sem, pr_sem, rs_sem, rr_sem, out_sem,
    zs_sem, zr_sem, as_sem, ar_sem, hs_sem, hr_sem, ys_sem, yr_sem, vs_sem, vr_sem, us_sem, ur_sem,
):
    sec = lax.axis_index("section")
    me = lax.axis_index("shard")
    rep = lax.axis_index("replica")
    x = me // 2
    c = me % 2
    mate = {"shard": x * 2 + 1 - c}
    other = {"section": 1 - sec}
    across_to = {"section": 1 - sec, "replica": flip(rep)}
    kinds = piece_kinds()

    def peer(d):
        return lax.rem(x + d, CHIPS)

    def at_peer(d):
        return {"shard": peer(d) * 2 + c}

    def at_rep(j):
        return {"replica": lax.rem(rep + j, REPL)}

    def at_shard(j):
        return {"shard": lax.rem(me + j, 8)}

    barrier = pltpu.get_barrier_semaphore()
    for j in range(1, REPL):
        pl.semaphore_signal(barrier, inc=1, device_id=at_shard(j), device_id_type=MESH)
        pl.semaphore_signal(barrier, inc=1, device_id=at_rep(j), device_id_type=MESH)
    for where in (other, across_to):
        pl.semaphore_signal(barrier, inc=1, device_id=where, device_id_type=MESH)
    pl.semaphore_wait(barrier, 16)

    def rows_of(chip):
        return pl.ds(pl.multiple_of(chip * ROWS, 32), ROWS)

    def w_src(kind, chip):
        if kind == 0:
            return vec_s
        if kind in (1, 5, 6):
            return wq_s.at[:, pl.ds(pl.multiple_of(QKV[kind] * D + chip * WO, WO), WO)]
        if kind == 2:
            return w1_s.at[:, pl.ds(pl.multiple_of(chip * W1, W1), W1)]
        return wo_s if kind == 3 else w2_s

    def w_dst(layer, kind, chip, core):
        if kind == 0:
            return vecs.at[layer, chip * 2 + core]
        if kind in (1, 2, 5, 6):
            rows = pl.ds(pl.multiple_of((chip * 2 + core) * 128, 128), 128)
            if kind == 2:
                return w1.at[layer, rows]
            return wq.at[layer, rows, pl.ds(QKV[kind] * WO, WO)]
        if kind == 3:
            return wo.at[layer, pl.ds(pl.multiple_of(core * 128, 128), 128)]
        return w2.at[layer, pl.ds(pl.multiple_of(core * 512, 512), 512)]

    def x_copy(kind, d, owner):
        return copy_to(
            w_src(kind, peer(d)), w_dst(sec, kind, owner, c), wxs.at[kind, d], wxr.at[kind, d], at_peer(d)
        )

    def own_piece(kind, d):
        return w_src(kind, x) if d == 0 else w_dst(sec, kind, peer(4 - d), c)

    def near_copy(kind, d, core):
        dst = w_dst(sec, kind, peer(4 - d), core)
        return copy_to(own_piece(kind, d), dst, wns.at[kind, d], wnr.at[kind, d], mate)

    yi = lax.rem(rep, 2)
    y_mate = {"replica": flip(rep)}

    def half_src(kind, h):
        if kind == 0:
            return vec_s
        size = 256 if kind == 4 else 64
        rows = pl.ds(pl.multiple_of(h * size, size), size)
        if kind in QKV:
            return wq_s.at[rows, pl.ds(pl.multiple_of(QKV[kind] * D + x * WO, WO), WO)]
        if kind == 2:
            return w1_s.at[rows, pl.ds(pl.multiple_of(x * W1, W1), W1)]
        return (wo_s if kind == 3 else w2_s).at[rows]

    def half_dst(layer, kind, d, h):
        chip = peer(4 - d)
        if kind == 0:
            return w_dst(layer, kind, chip, c)
        size = 256 if kind == 4 else 64
        base = c if kind in (3, 4) else chip * 2 + c
        rows = pl.ds(pl.multiple_of((base * 2 + h) * size, size), size)
        if kind in QKV:
            return wq.at[layer, rows, pl.ds(QKV[kind] * WO, WO)]
        return {2: w1, 3: wo, 4: w2}[kind].at[layer, rows]

    def across_copy(kind, d, layer, h):
        src = half_src(kind, h) if d == 0 else half_dst(sec, kind, d, h)
        return copy_to(src, half_dst(layer, kind, d, h), was.at[kind, d], war.at[kind, d], across_to)

    def pass_copy(kind, d, h):
        ref = half_dst(1 - sec, kind, d, h)
        return copy_to(ref, ref, wys.at[kind, d], wyr.at[kind, d], y_mate)

    def far_copy(kind, d, core):
        ref = w_dst(1 - sec, kind, peer(4 - d), core)
        return copy_to(ref, ref, wfs.at[kind, d], wfr.at[kind, d], mate)

    def local_copy(kind):
        return pltpu.make_async_copy(w_src(kind, x), w_dst(sec, kind, x, c), loc_sem.at[kind])

    def launch(kind):
        if kind not in (3, 4):
            for d in (1, 3, 2):
                x_copy(kind, d, x).start()
        near_copy(kind, 0, c).start()
        across_copy(kind, 0, sec, yi).start()
        local_copy(kind).start()

    def settle_near(kind):
        for d in kinds[kind][1:]:
            x_copy(kind, d, peer(4 - d)).wait_recv()
            near_copy(kind, d, c).start()
            across_copy(kind, d, sec, yi).start()
        local_copy(kind).wait()
        for d in kinds[kind]:
            near_copy(kind, d, 1 - c).wait_recv()

    def far_in(kind):
        for d in kinds[kind]:
            across_copy(kind, d, 1 - sec, 1 - yi).wait_recv()
            if kind != 0:
                pass_copy(kind, d, 1 - yi).start()

    def far_on(kind):
        for d in kinds[kind]:
            if kind != 0:
                pass_copy(kind, d, yi).wait_recv()
            far_copy(kind, d, c).start()

    def far_done(kind):
        for d in kinds[kind]:
            far_copy(kind, d, 1 - c).wait_recv()

    swap_copy = copy_to(bnd.at[1 - sec], swap, cs_sem.at[0], cr_sem.at[0], other)
    carry_copy = copy_to(carry_s, carry_r, cs_sem.at[1], cr_sem.at[1], other)

    at = 0
    for v in (v_ln1g, v_ln1b, v_qv, v_out, v_ln2g, v_ln2b, v_fc1, v_fc2):
        for t in range(v.shape[1] // 128):
            vec_s[at : at + 1, :] = v[:, t * 128 : t * 128 + 128].astype(F32)
            at += 1
    launch(0)
    swap_copy.start()
    for kind in QKV:
        launch(kind)
    idc[...] = jnp.transpose(jnp.broadcast_to(idr[:1, :], (128, KEYS)))
    settle_near(0)

    @pl.when(sec == 0)
    def _():
        rin[0] = bnd[0].astype(F32)

    @pl.when(sec == 1)
    def _():
        far_in(0)
        far_on(0)
        far_done(0)
        swap_copy.wait_recv()
        rin[0] = swap[...].astype(F32)
        gnext[...] = bnd[1].astype(F32)

    def vec_row(l, k):
        return jnp.concatenate([vecs[l, i, k : k + 1, :] for i in range(8)], axis=1)

    def pieces(l, i, ks):
        part = vecs[l, i]
        return [part[k : k + 1, :] for k in ks]

    def gather_copy(buf, kind, l, d, owner):
        ref = buf.at[l, rows_of(owner)]
        return copy_to(ref, ref, xs_sem.at[kind, l, d], xr_sem.at[kind, l, d], at_peer(d))

    def scatter_copy(kind, l, d):
        return copy_to(
            stage.at[d - 1],
            landed.at[kind // 2, d - 1],
            xs_sem.at[kind, l, d],
            xr_sem.at[kind, l, d],
            at_peer(d),
        )

    def gather_start(buf, kind, l):
        for d in (1, 3, 2):
            gather_copy(buf, kind, l, d, x).start()

    def gather_wait(buf, kind, l, d):
        gather_copy(buf, kind, l, d, peer(4 - d)).wait_recv()

    def scatter_add(kind, l, base):
        total = base
        for d in (1, 3, 2):
            scatter_copy(kind, l, d).wait_recv()
            total = total + landed[kind // 2, d - 1].astype(F32)
        for d in (1, 3, 2):
            scatter_copy(kind, l, d).wait_send()
        return total

    def send_part(kind, l, d, part):
        @pl.when(d == 0)
        def _():
            own[...] = part

        @pl.when(d != 0)
        def _():
            stage[d - 1] = part.astype(BF16)
            scatter_copy(kind, l, d).start()

    def kv_copy(l, d):
        rows = rows_of(peer(4 - d))
        return copy_to(
            qkv.at[l, rows, pl.ds(WO, 2 * WO)], kvp.at[l, rows], ks_sem.at[l, d], kr_sem.at[l, d], mate
        )

    lane = lax.broadcasted_iota(jnp.int32, (1, 128), 1)

    def forward(l, first):
        lower = (l == 0) & (sec == 0)
        upper = (l == 0) & (sec == 1)
        qkv_b = jnp.concatenate(
            pieces(l, x, (2, 3)) + [jnp.zeros((1, WO), F32)] + pieces(l, 4 + x, (2, 3)), axis=1
        )
        fc1_b = jnp.concatenate(
            pieces(l, 2 * x, (7, 8, 9, 10)) + pieces(l, 2 * x + 1, (7, 8, 9, 10)), axis=1
        )
        normed, _ = norm_parts(rin[l])
        n1[l, rows_of(x)] = (normed * vec_row(l, 0) + vec_row(l, 1)).astype(BF16)
        gather_start(n1, AG1, l)

        @pl.when(l == 0)
        def _():
            for kind in QKV:
                settle_near(kind)
            launch(3)
            launch(2)
            launch(4)

        @pl.when(upper)
        def _():
            for step in (far_in, far_on, far_done):
                for kind in QKV:
                    step(kind)

        def project(k, _):
            d = gray(k)
            rows = rows_of(peer(4 - d))

            @pl.when(d != 0)
            def _():
                gather_wait(n1, AG1, l, d)

            qkv[l, rows] = (mm(n1[l, rows], wq[l]) + qkv_b).astype(BF16)
            kv_copy(l, d).start()
            return 0

        lax.fori_loop(0, CHIPS, project, 0)

        @pl.when(l == 0)
        def _():
            settle_near(3)

        @pl.when(upper)
        def _():
            far_in(3)
            far_on(3)
            far_done(3)

        for d in range(CHIPS):
            kv_copy(l, d).wait_recv()

        def attend(j, _):
            d = gray(lax.rem(j + 1, CHIPS))
            rows = rows_of(peer(d))
            bias = jnp.where(idc[rows][:, :1] == idr[:1, :], 0.0, NEG)
            for pair in range(2):
                lanes = slice(pair * 128, pair * 128 + 128)
                q = qkv[l, rows, lanes] * jnp.asarray(HEAD**-0.5, BF16)
                k_own = qkv[l, :, WO + pair * 128 : WO + pair * 128 + 128]
                v_own = qkv[l, :, 2 * WO + pair * 128 : 2 * WO + pair * 128 + 128]
                k_par = kvp[l, :, lanes]
                v_par = kvp[l, :, WO + pair * 128 : WO + pair * 128 + 128]
                outs = []
                for half in range(2):
                    qm = jnp.where(lane // HEAD == half, q, jnp.zeros_like(q))
                    s = jnp.concatenate([mm_t(qm, k_own), mm_t(qm, k_par)], axis=1) + bias
                    p = jnp.exp(s - jnp.max(s, axis=1, keepdims=True))
                    scale = 1.0 / jnp.sum(p, axis=1, keepdims=True)
                    p = p.astype(BF16)
                    outs.append((mm(p[:, :TOK], v_own) + mm(p[:, TOK:], v_par)) * scale)
                wt[l, rows, lanes] = jnp.where(lane < HEAD, outs[0], outs[1]).astype(BF16)
            send_part(RS1, l, d, mm(wt[l, rows], wo[l]))
            return 0

        lax.fori_loop(0, CHIPS, attend, 0)

        @pl.when(l == 0)
        def _():
            settle_near(2)

        @pl.when(upper)
        def _():
            far_in(2)
            far_in(4)

        rmid[l] = rin[l] + (scatter_add(RS1, l, own[...]) + vec_row(l, 4))
        normed, _ = norm_parts(rmid[l])
        n2[l, rows_of(x)] = (normed * vec_row(l, 5) + vec_row(l, 6)).astype(BF16)
        gather_start(n2, AG2, l)

        @pl.when(l == 0)
        def _():
            settle_near(4)

        @pl.when(upper)
        def _():
            for step in (far_on, far_done):
                step(2)
                step(4)

        @pl.when(lower)
        def _():
            swap_copy.wait_recv()
            gnext[...] = swap[...].astype(F32)
            for kind in (0, 1, 5, 6, 3, 2, 4):
                far_in(kind)

        def feed(k, _):
            d = gray(k)
            back = lax.rem(4 - d, CHIPS)
            rows = rows_of(peer(back))

            @pl.when(d != 0)
            def _():
                gather_wait(n2, AG2, l, d)

            h = mm(n2[l, rows], w1[l]) + fc1_b
            phi = 0.5 + 0.5 * lax.erf(h * (0.5**0.5))
            act[l, rows] = (h * phi).astype(BF16)
            dgl[l, rows] = phi + h * (jnp.exp(-0.5 * h * h) * 0.3989422804014327)
            send_part(RS2, l, back, mm(act[l, rows], w2[l]))
            return 0

        lax.fori_loop(0, CHIPS, feed, 0)

        @pl.when(lower)
        def _():
            for step in (far_on, far_done):
                for kind in (0, 1, 5, 6, 3, 2, 4):
                    step(kind)

        out = rmid[l] + (scatter_add(RS2, l, own[...]) + vec_row(l, 11))

        @pl.when(l == 0)
        def _():
            rin[1] = out.astype(BF16).astype(F32)

        @pl.when((l == 1) & (sec == 0))
        def _():
            carry_s[...] = out.astype(BF16)
            carry_copy.start()

        @pl.when((l == 1) & (sec == 1))
        def _():
            edge_o[1] = out

        return first

    lax.fori_loop(0, 2, forward, 0)

    vg_o[...] = jnp.zeros_like(vg_o)

    def col_sum(v):
        return jnp.sum(v, axis=0, keepdims=True)

    def dkv_copy(l):
        return copy_to(dkv_s.at[l], dkv_r.at[l], ds_sem.at[l], dr_sem.at[l], mate)

    def grads_mlp(l):
        def block(t, _):
            cols = pl.ds(pl.multiple_of(t * 256, 256), 256)
            pgb[t] = over_rows(n2[l, :, cols], dh[l]).astype(BF16).reshape(2, 128, W1)
            half = pl.ds(pl.multiple_of(lax.rem(t, 2) * 256, 256), 256)
            pgd[t // 2, half] = over_rows(act[l, :, cols], g[l]).astype(BF16)
            return 0

        lax.fori_loop(0, CHIPS, block, 0)

    def grads_att(l):
        def block(t, _):
            cols = pl.ds(pl.multiple_of(t * 256, 256), 256)
            pga[t] = over_rows(n1[l, :, cols], dp[l]).astype(BF16).reshape(2, 128, WQ)
            return 0

        lax.fori_loop(0, CHIPS, block, 0)
        pgc[...] = over_rows(wt[l], ga[l]).astype(BF16).reshape(2, 128, D)

    def pair_mlp(l):
        return (
            copy_to(pgb.at[:, 1 - c], rgb, ps_sem.at[l, 1], pr_sem.at[l, 1], mate),
            copy_to(pgd.at[1 - c], rgd, ps_sem.at[l, 3], pr_sem.at[l, 3], mate),
        )

    def pair_att(l):
        return (
            copy_to(pga.at[:, 1 - c], rga, ps_sem.at[l, 0], pr_sem.at[l, 0], mate),
            copy_to(pgc.at[1 - c], rgc, ps_sem.at[l, 2], pr_sem.at[l, 2], mate),
        )

    def piece_of(l, r):
        return r + (l + sec - 2 * l * sec) * (1 - 2 * lax.rem(r, 2))

    def few(p):
        return pl.ds(pl.multiple_of(p * 16, 16), 16)

    def more(p):
        return pl.ds(pl.multiple_of(p * 64, 64), 64)

    def spread_copy(l, n, j):
        p = piece_of(l, lax.rem(rep + j, REPL))
        src = (rga.at[:, few(p)], rgb.at[:, few(p)], rgc.at[few(p)], rgd.at[more(p)])[n]
        return copy_to(src, (lga, lgb, lgc, lgd)[n].at[l, j], rs_sem.at[l, n, j], rr_sem.at[l, n, j], at_rep(j))

    def each_piece(l, ns, act_on):
        def one(j, _):
            for n in ns:
                act_on(spread_copy(l, n, j))
            return 0

        lax.fori_loop(1, REPL, one, 0)

    def sent(cp):
        cp.wait_send()

    def arrived(cp):
        cp.wait_recv()

    def begin(cp):
        cp.start()

    def both(u, v):
        return (u.astype(F32) + v.astype(F32)).astype(BF16)

    def spread_mlp(l):
        for cp in pair_mlp(l):
            cp.wait_recv()
        for t in range(CHIPS):
            rgb[t] = both(pgb[t, c], rgb[t])
        rgd[...] = both(pgd[c], rgd[...])
        p = piece_of(l, rep)
        for t in range(CHIPS):
            em[l, t * 16 : t * 16 + 16] = rgb[t, few(p)].astype(F32)
        em[l, 64:] = rgd[more(p)].astype(F32)
        each_piece(l, (1, 3), begin)

    def spread_att(l):
        for cp in pair_att(l):
            cp.wait_recv()
        for t in range(CHIPS):
            rga[t] = both(pga[t, c], rga[t])
        rgc[...] = both(pgc[c], rgc[...])
        p = piece_of(l, rep)
        for t in range(CHIPS):
            ea[l, t * 16 : t * 16 + 16] = rga[t, few(p)].astype(F32)
        ec[l] = rgc[few(p)].astype(F32)
        each_piece(l, (0, 2), begin)

    def collect_mlp(l):
        each_piece(l, (1, 3), arrived)
        for t in range(CHIPS):
            rows = slice(t * 16, t * 16 + 16)
            total = em[l, rows]
            for j in range(1, REPL):
                total = total + lgb[l, j, t].astype(F32)
            em[l, rows] = total
        total = em[l, 64:]
        for j in range(1, REPL):
            total = total + lgd[l, j].astype(F32)
        em[l, 64:] = total

    def collect_att(l):
        each_piece(l, (0, 2), arrived)
        for t in range(CHIPS):
            rows = slice(t * 16, t * 16 + 16)
            total = ea[l, rows]
            for j in range(1, REPL):
                total = total + lga[l, j, t].astype(F32)
            ea[l, rows] = total
        total = ec[l]
        for j in range(1, REPL):
            total = total + lgc[l, j].astype(F32)
        ec[l] = total

    def backward(i, first):
        l = 1 - i

        def add_vec(k, v):
            vg_o[l, k : k + 1, : v.shape[1]] += v

        def norm_back(v, gain, dy, k):
            xhat, rstd = norm_parts(v)
            add_vec(k, col_sum(dy * xhat))
            add_vec(k + 1, col_sum(dy))
            dyg = dy * gain
            return rstd * (
                dyg - jnp.mean(dyg, axis=-1, keepdims=True) - xhat * jnp.mean(dyg * xhat, axis=-1, keepdims=True)
            )

        low = gnext[...].astype(BF16)
        g[l, rows_of(x)] = low
        gather_start(g, BAG1, l)
        add_vec(7, col_sum(low.astype(F32)))

        @pl.when(i == 1)
        def _():
            grads_att(1)
            each_piece(1, (1, 3), sent)
            for cp in pair_att(1):
                cp.start()
            collect_mlp(1)

        def feed(k, _):
            d = gray(k)
            back = lax.rem(4 - d, CHIPS)
            rows = rows_of(peer(back))

            @pl.when(d != 0)
            def _():
                gather_wait(g, BAG1, l, d)

            d_low = (mm_t(g[l, rows], w2[l]) * dgl[l, rows]).astype(BF16)
            dh[l, rows] = d_low
            add_vec(6, col_sum(d_low.astype(F32)))
            send_part(BRS1, l, back, mm_t(d_low, w1[l]))
            return 0

        lax.fori_loop(0, CHIPS, feed, 0)

        @pl.when(i == 1)
        def _():
            spread_att(1)
            for cp in pair_mlp(1):
                cp.wait_send()

        grads_mlp(l)
        for cp in pair_mlp(l):
            cp.start()
        dn2 = scatter_add(BRS1, l, own[...])
        d_mid = gnext[...] + norm_back(rmid[l], vec_row(l, 5), dn2, 4)
        rmid[l] = d_mid
        low = d_mid.astype(BF16)
        ga[l, rows_of(x)] = low
        gather_start(ga, BAG2, l)
        add_vec(3, col_sum(low.astype(F32)))

        def expand(k, _):
            d = gray(k)
            rows = rows_of(peer(4 - d))

            @pl.when(d != 0)
            def _():
                gather_wait(ga, BAG2, l, d)

            dw[rows] = mm_t(ga[l, rows], wo[l]).astype(BF16)
            return 0

        lax.fori_loop(0, CHIPS, expand, 0)
        spread_mlp(l)
        dkv[...] = jnp.zeros_like(dkv)

        def attend(b, _):
            rows = pl.ds(pl.multiple_of(b * 128, 128), 128)
            bias = jnp.where(idc[:, :1] == idr[:, rows][:1, :], 0.0, NEG)
            for pair in range(2):
                lanes = slice(pair * 128, pair * 128 + 128)
                q = qkv[l, rows, lanes] * jnp.asarray(HEAD**-0.5, BF16)
                do = dw[rows, lanes]
                k_all = jnp.concatenate(
                    [qkv[l, :, WO + pair * 128 : WO + pair * 128 + 128], kvp[l, :, lanes]], axis=0
                )
                v_all = jnp.concatenate(
                    [
                        qkv[l, :, 2 * WO + pair * 128 : 2 * WO + pair * 128 + 128],
                        kvp[l, :, WO + pair * 128 : WO + pair * 128 + 128],
                    ],
                    axis=0,
                )
                dqs = []
                for half in range(2):
                    keep = lane // HEAD == half
                    qm = jnp.where(keep, q, jnp.zeros_like(q))
                    dom = jnp.where(keep, do, jnp.zeros_like(do))
                    s = mm_t(k_all, qm) + bias
                    p = jnp.exp(s - jnp.max(s, axis=0, keepdims=True))
                    p = p * (1.0 / jnp.sum(p, axis=0, keepdims=True))
                    dpr = mm_t(v_all, dom)
                    ds = (p * (dpr - jnp.sum(p * dpr, axis=0, keepdims=True))).astype(BF16)
                    dkv[:, lanes] += mm(ds, qm)
                    dkv[:, WO + pair * 128 : WO + pair * 128 + 128] += mm(p.astype(BF16), dom)
                    dqs.append(over_rows(ds, k_all))
                dq = jnp.where(lane < HEAD, dqs[0], dqs[1]) * (HEAD**-0.5)
                dp[l, rows, lanes] = dq.astype(BF16)
            return 0

        lax.fori_loop(0, TOK // 128, attend, 0)
        dkv_s[l] = dkv[TOK:].astype(BF16)

        @pl.when(i == 1)
        def _():
            collect_att(1)
            each_piece(1, (0, 2), sent)

        dkv_copy(l).start()
        dkv_copy(l).wait_recv()
        dp[l, :, WO:] = (dkv[:TOK] + dkv_r[l].astype(F32)).astype(BF16)
        add_vec(
            2,
            jnp.concatenate(
                [col_sum(dp[l, :, :WO].astype(F32)), col_sum(dp[l, :, 2 * WO :].astype(F32))], axis=1
            ),
        )

        @pl.when(i == 1)
        def _():
            for cp in pair_att(1):
                cp.wait_send()
            grads_att(0)
            for cp in pair_att(0):
                cp.start()

        def shrink(j, _):
            d = gray(lax.rem(j + 1, CHIPS))
            send_part(BRS2, l, d, mm_t(dp[l, rows_of(peer(d))], wq[l]))
            return 0

        lax.fori_loop(0, CHIPS, shrink, 0)

        @pl.when(i == 1)
        def _():
            spread_att(0)

        dn1 = scatter_add(BRS2, l, own[...])
        d_in = rmid[l] + norm_back(rin[l], vec_row(l, 0), dn1, 0)

        @pl.when(i == 0)
        def _():
            gnext[...] = d_in.astype(BF16).astype(F32)

        @pl.when((i == 1) & (sec == 1))
        def _():
            carry_s[...] = d_in.astype(BF16)
            carry_copy.start()

        @pl.when((i == 1) & (sec == 0))
        def _():
            edge_o[0] = d_in

        return first

    lax.fori_loop(0, 2, backward, 0)

    def vec_copy(j):
        return copy_to(vg_o, lv.at[j], vs_sem.at[j], vr_sem.at[j], at_rep(j))

    def vec_share(j, slot):
        return copy_to(tv, fv.at[slot], us_sem.at[j], ur_sem.at[j], at_shard(j))

    def cross_copy(n):
        src, dst = ((zm, ym), (za, ya), (zc, yc), (zv, yv))[n]
        return copy_to(src, dst, zs_sem.at[n], zr_sem.at[n], across_to)

    def turn_refs(n, source):
        if n == 0:
            return pm, q1.at[:, pl.ds(pl.multiple_of(source * W1, W1), W1)]
        return pa, qt.at[few(source)]

    def turn_copy(n, d, source):
        src, dst = turn_refs(n, source)
        return copy_to(src.at[few(peer(d))], dst, as_sem.at[n, d], ar_sem.at[n, d], at_peer(d))

    def turn_start(n):
        for d in (1, 3, 2):
            turn_copy(n, d, x).start()
        src, dst = turn_refs(n, x)
        dst[...] = src[few(x)]

    def turn_wait(n):
        for d in (1, 3, 2):
            turn_copy(n, d, peer(4 - d)).wait_recv()

    zi = rep // 2
    pieces_of = ((q1, f1), (qa, fa), (pc, fc), (p2, f2))

    def slot_ref(n, slot):
        return pieces_of[n][1].at[more(slot) if n == 3 else few(slot)]

    def slot_of(d, y):
        return lax.rem(zi + 4 - d, 4) * 2 + y

    def along_z(n, d, slot):
        src = pieces_of[n][0]
        where = {"replica": lax.rem(zi + d, 4) * 2 + yi}
        return copy_to(src, slot_ref(n, slot), hs_sem.at[n, d], hr_sem.at[n, d], where)

    def along_z_late(n, d, slot):
        ref = slot_ref(n, slot)
        where = {"replica": lax.rem(zi + d, 4) * 2 + yi}
        return copy_to(ref, ref, hs_sem.at[n, 4 + d], hr_sem.at[n, 4 + d], where)

    def along_y(n, d, y):
        dst = slot_ref(n, slot_of(d, y))
        return copy_to(pieces_of[n][0] if d == 0 else dst, dst, ys_sem.at[n, d], yr_sem.at[n, d], y_mate)

    def keep_piece(n):
        return pltpu.make_async_copy(pieces_of[n][0], slot_ref(n, rep), out_sem.at[n])

    def share_start(n):
        along_y(n, 0, yi).start()
        for d in (1, 3, 2):
            along_z(n, d, rep).start()
        keep_piece(n).start()

    def share_on(n):
        if n in (2, 3):
            along_y(n, 0, 1 - yi).wait_recv()
            for d in (1, 3, 2):
                along_z_late(n, d, flip(rep)).start()
            return
        for d in (1, 3, 2):
            along_z(n, d, slot_of(d, yi)).wait_recv()
            along_y(n, d, yi).start()

    for j in range(1, REPL):
        vec_copy(j).start()
    collect_mlp(0)
    zm[...] = em[1 - sec].astype(BF16)
    cross_copy(0).start()
    total = vg_o[...]
    for j in range(1, REPL):
        vec_copy(j).wait_recv()
        total = total + lv[j]
    vg_o_sum = total
    zv[...] = jnp.where(sec == 0, vg_o_sum[1], vg_o_sum[0])
    cross_copy(3).start()
    cross_copy(0).wait_recv()
    pm[...] = (em[sec, :64] + ym[:64].astype(F32)).astype(BF16)
    p2[...] = (em[sec, 64:] + ym[64:].astype(F32)).astype(BF16)
    turn_start(0)
    share_start(3)
    turn_wait(0)
    share_start(0)
    share_on(3)
    collect_att(0)
    za[...] = ea[1 - sec].astype(BF16)
    zc[...] = ec[1 - sec].astype(BF16)
    cross_copy(1).start()
    cross_copy(2).start()
    cross_copy(3).wait_recv()
    tv[...] = jnp.where(sec == 0, vg_o_sum[0], vg_o_sum[1]) + yv[...]
    fv[me] = tv[...]
    for j in range(1, REPL):
        vec_share(j, me).start()
    cross_copy(1).wait_recv()
    cross_copy(2).wait_recv()
    pa[...] = (ea[sec] + ya[...].astype(F32)).astype(BF16)
    pc[...] = (ec[sec] + yc[...].astype(F32)).astype(BF16)
    turn_start(1)
    share_start(2)
    turn_wait(1)
    for t in range(3):
        for chip in range(CHIPS):
            at = t * D + chip * WO
            qa[:, at : at + WO] = qt[chip * 16 : chip * 16 + 16, t * WO : t * WO + WO]
    share_start(1)
    share_on(0)
    share_on(2)
    share_on(1)
    for n in range(4):
        if n in (2, 3):
            for d in (1, 3, 2):
                along_z(n, d, slot_of(d, yi)).wait_recv()
                along_z_late(n, d, slot_of(d, 1 - yi)).wait_recv()
        else:
            for d in range(4):
                along_y(n, d, 1 - yi).wait_recv()
        keep_piece(n).wait()
    for j in range(1, REPL):
        vec_share(j, lax.rem(me + 8 - j, 8)).wait_recv()

    carry_copy.wait_recv()
    edge_o[1 - sec] = carry_r[...].astype(F32)
    carry_copy.wait_send()
    swap_copy.wait_send()
    for kind in kinds:
        for d in kinds[kind]:
            if d != 0:
                x_copy(kind, d, x).wait_send()
            near_copy(kind, d, c).wait_send()
            across_copy(kind, d, sec, yi).wait_send()
            if kind != 0:
                pass_copy(kind, d, 1 - yi).wait_send()
            far_copy(kind, d, c).wait_send()
    for l in range(2):
        for d in (1, 2, 3):
            for buf, kind in ((n1, AG1), (n2, AG2), (g, BAG1), (ga, BAG2)):
                gather_copy(buf, kind, l, d, x).wait_send()
        for d in range(CHIPS):
            kv_copy(l, d).wait_send()
        dkv_copy(l).wait_send()
    each_piece(0, (0, 1, 2, 3), sent)
    for cp in pair_mlp(0) + pair_att(0):
        cp.wait_send()
    for n in range(4):
        cross_copy(n).wait_send()
    for n in range(2):
        for d in (1, 2, 3):
            turn_copy(n, d, x).wait_send()
    for n in range(4):
        for d in (1, 2, 3):
            along_z(n, d, rep).wait_send()
            if n in (2, 3):
                along_z_late(n, d, flip(rep)).wait_send()
        for d in range(1 if n in (2, 3) else 4):
            along_y(n, d, yi).wait_send()
    for j in range(1, REPL):
        vec_copy(j).wait_send()
        vec_share(j, me).wait_send()


def run_step(*operands):
    vm = pl.BlockSpec(memory_space=pltpu.VMEM)
    hbm = pl.BlockSpec(memory_space=pl.ANY)
    sds = jax.ShapeDtypeStruct
    dma = pltpu.SemaphoreType.DMA
    return pl.pallas_call(
        step_kernel,
        out_shape=(
            sds((MICRO, ROWS, D), F32),
            sds((8, 8, D), F32),
            sds((128, FF), BF16),
            sds((128, 3 * D), BF16),
            sds((128, D), BF16),
            sds((512, D), BF16),
        ),
        in_specs=[vm] * 10 + [hbm] * 4,
        out_specs=(vm, vm, hbm, hbm, hbm, hbm),
        scratch_shapes=[
            pltpu.VMEM((KEYS, 128), jnp.int32),
            pltpu.VMEM((16, 128), F32),
            pltpu.VMEM((2, 8, 16, 128), F32),
            pltpu.VMEM((2, D, WQ), BF16),
            pltpu.VMEM((2, WO, D), BF16),
            pltpu.VMEM((2, D, W1), BF16),
            pltpu.VMEM((2, W1, D), BF16),
            pltpu.VMEM((2, TOK, D), BF16),
            pltpu.VMEM((2, TOK, D), BF16),
            pltpu.VMEM((2, TOK, W1), BF16),
            pltpu.VMEM((2, TOK, W1), F32),
            pltpu.VMEM((2, TOK, WQ), BF16),
            pltpu.VMEM((2, TOK, 2 * WO), BF16),
            pltpu.VMEM((2, TOK, WO), BF16),
            pltpu.VMEM((2, ROWS, D), F32),
            pltpu.VMEM((2, ROWS, D), F32),
            pltpu.VMEM((2, TOK, D), BF16),
            pltpu.VMEM((2, TOK, D), BF16),
            pltpu.VMEM((2, TOK, W1), BF16),
            pltpu.VMEM((2, TOK, WQ), BF16),
            pltpu.VMEM((TOK, WO), BF16),
            pltpu.VMEM((3, ROWS, D), BF16),
            pltpu.VMEM((4, 3, ROWS, D), BF16),
            pltpu.VMEM((ROWS, D), BF16),
            pltpu.VMEM((ROWS, D), BF16),
            pltpu.VMEM((ROWS, D), BF16),
            pltpu.VMEM((KEYS, 2 * WO), F32),
            pltpu.VMEM((2, TOK, 2 * WO), BF16),
            pltpu.VMEM((2, TOK, 2 * WO), BF16),
            pltpu.VMEM((ROWS, D), F32),
            pltpu.VMEM((ROWS, D), F32),
            pltpu.VMEM((CHIPS, 2, 128, WQ), BF16),
            pltpu.VMEM((CHIPS, 2, 128, W1), BF16),
            pltpu.VMEM((2, 128, D), BF16),
            pltpu.VMEM((2, 512, D), BF16),
            pltpu.VMEM((CHIPS, 128, WQ), BF16),
            pltpu.VMEM((CHIPS, 128, W1), BF16),
            pltpu.VMEM((128, D), BF16),
            pltpu.VMEM((512, D), BF16),
            pltpu.VMEM((2, REPL, CHIPS, 16, WQ), BF16),
            pltpu.VMEM((2, REPL, CHIPS, 16, W1), BF16),
            pltpu.VMEM((2, REPL, 16, D), BF16),
            pltpu.VMEM((2, REPL, 64, D), BF16),
            pltpu.VMEM((2, 8, D), F32),
            pltpu.VMEM((2, 128, D), F32),
            pltpu.VMEM((2, 64, WQ), F32),
            pltpu.VMEM((2, 16, D), F32),
            pltpu.VMEM((128, D), BF16),
            pltpu.VMEM((64, WQ), BF16),
            pltpu.VMEM((16, D), BF16),
            pltpu.VMEM((128, D), BF16),
            pltpu.VMEM((64, WQ), BF16),
            pltpu.VMEM((16, D), BF16),
            pltpu.VMEM((64, D), BF16),
            pltpu.VMEM((64, D), BF16),
            pltpu.VMEM((64, WQ), BF16),
            pltpu.VMEM((16, D), BF16),
            pltpu.VMEM((16, FF), BF16),
            pltpu.VMEM((64, WQ), BF16),
            pltpu.VMEM((16, 3 * D), BF16),
            pltpu.VMEM((REPL, 2, 8, D), F32),
            pltpu.VMEM((8, D), F32),
            pltpu.VMEM((8, D), F32),
            pltpu.VMEM((8, D), F32),
            dma((8, 2, CHIPS)),
            dma((8, 2, CHIPS)),
            dma((2, CHIPS)),
            dma((2, CHIPS)),
            dma((2,)),
            dma((2,)),
            dma((2,)),
            dma((2,)),
            dma((7, CHIPS)),
            dma((7, CHIPS)),
            dma((7, CHIPS)),
            dma((7, CHIPS)),
            dma((7, CHIPS)),
            dma((7, CHIPS)),
            dma((7, CHIPS)),
            dma((7, CHIPS)),
            dma((7, CHIPS)),
            dma((7, CHIPS)),
            dma((7,)),
            dma((2, 4)),
            dma((2, 4)),
            dma((2, 4, REPL)),
            dma((2, 4, REPL)),
            dma((4,)),
            dma((4,)),
            dma((4,)),
            dma((2, CHIPS)),
            dma((2, CHIPS)),
            dma((4, 8)),
            dma((4, 8)),
            dma((4, 4)),
            dma((4, 4)),
            dma((REPL,)),
            dma((REPL,)),
            dma((REPL,)),
            dma((REPL,)),
        ],
        compiler_params=pltpu.CompilerParams(
            collective_id=0, has_side_effects=True, vmem_limit_bytes=62 * 1024 * 1024
        ),
    )(*operands)


def body(
    boundary, image_of_token, ln1_gain, ln1_bias, w_qkv, qv_bias, w_out, out_bias,
    ln2_gain, ln2_bias, w_fc1, fc1_bias, w_fc2, fc2_bias,
):
    me = lax.axis_index("shard")
    x, c = me // 2, me % 2
    sec = lax.axis_index("section")
    bnd = boundary[0, :, 0]
    ids = lax.dynamic_index_in_dim(image_of_token[:, 0], sec, 0, keepdims=False).reshape(CHIPS, 2, ROWS)
    flipped = jnp.where(c == 0, ids, ids[:, ::-1])
    ids = jnp.swapaxes(flipped, 0, 1).reshape(KEYS)
    idr = jnp.broadcast_to(ids[None, :], (8, KEYS))
    edge, fv, f1, fa, fc, f2 = run_step(
        bnd, idr, ln1_gain, ln1_bias, qv_bias, out_bias, ln2_gain, ln2_bias, fc1_bias, fc2_bias,
        w_qkv[0], w_out[0], w_fc1[0], w_fc2[0],
    )
    g_qkv, g_fc1, g_out, g_fc2 = (v.astype(F32) for v in (fa, f1, fc, f2))

    whole = jnp.sum(fv, axis=0)
    pairs = jnp.sum(fv.reshape(CHIPS, 2, 8, D), axis=1)
    wide = jnp.concatenate(
        [whole[k] for k in (0, 1, 3, 4, 5, 7)]
        + [pairs[:, 2, :WO].reshape(-1), pairs[:, 2, WO : 2 * WO].reshape(-1), pairs[:, 6].reshape(-1)]
    )

    def part(at, size):
        return lax.dynamic_slice_in_dim(wide, at + me * size, size)[None]

    return (
        edge[None, :, None],
        part(0, 128),
        part(1024, 128),
        g_qkv[None],
        part(6 * D, 256),
        g_out[None],
        part(2 * D, 128),
        part(3 * D, 128),
        part(4 * D, 128),
        g_fc1[None],
        part(8 * D, 512),
        g_fc2[None],
        part(5 * D, 128),
    )


def solution(mesh):
    row = P("section", "shard")
    mat = P("section", "shard", None)
    edge = P("section", None, "replica", "shard", None)
    in_specs = (edge, P(None, "replica", None), row, row, mat, row, mat, row, row, row, mat, row, mat, row)
    out_specs = (edge, row, row, mat, row, mat, row, row, row, mat, row, mat, row)
    return jax.shard_map(body, mesh=mesh, in_specs=in_specs, out_specs=out_specs, check_vma=False)
```

```python
import functools

import jax
import jax.numpy as jnp
from jax import lax
from jax.experimental import pallas as pl
from jax.experimental.pallas import tpu as pltpu
from jax.sharding import PartitionSpec as P

D = 1024
HEADS = 16
HEAD = 64
FF = 4096
EPS = 1e-06
NEG = -1e30

MICRO = 2
CHIPS = 4
ROWS = 96
TOK = CHIPS * ROWS
KEYS = 2 * TOK
WQ = 3 * D // CHIPS
WO = D // CHIPS
W1 = FF // CHIPS
REPL = 8

MESH = pl.DeviceIdType.MESH
F32 = jnp.float32
BF16 = jnp.bfloat16

AG1, RS1, AG2, RS2, BAG1, BRS1, BAG2, BRS2 = range(8)


def mm(a, b):
    return jnp.dot(a, b, preferred_element_type=F32)


def mm_t(a, b):
    return lax.dot_general(a, b, (((1,), (1,)), ((), ())), preferred_element_type=F32)


def over_rows(a, b):
    return lax.dot_general(a, b, (((0,), (0,)), ((), ())), preferred_element_type=F32)


def norm_parts(v):
    centered = v - jnp.mean(v, axis=-1, keepdims=True)
    rstd = lax.rsqrt(jnp.mean(centered * centered, axis=-1, keepdims=True) + EPS)
    return centered * rstd, rstd


def gray(k):
    return k + k // 2 - 2 * (k // 3)


def flip(r):
    return r + 1 - 2 * lax.rem(r, 2)


def copy_to(src, dst, send, recv, where):
    return pltpu.make_async_remote_copy(
        src_ref=src, dst_ref=dst, send_sem=send, recv_sem=recv, device_id=where, device_id_type=MESH
    )


QKV = {1: 0, 5: 1, 6: 2}


def piece_kinds():
    table = {kind: (0, 1, 3, 2) for kind in (0, 1, 2, 5, 6)}
    table.update({3: (0,), 4: (0,)})
    return table


def step_kernel(
    bnd, idr, v_ln1g, v_ln1b, v_qv, v_out, v_ln2g, v_ln2b, v_fc1, v_fc2, wq_s, wo_s, w1_s, w2_s,
    edge_o, vo, f1, fa, fc, f2,
    fv, idc, vec_s, vecs, wq, wo, w1, w2,
    n1, n2, act, dgl, qkv, kvp, wt, rin, rmid, g, ga, dh, dp, dw,
    stage, landed, swap, carry_s, carry_r, dkv, dkv_s, dkv_r, own, gnext,
    pga, pgb, pgc, pgd, rga, rgb, rgc, rgd, lga, lgb, lgc, lgd,
    vg_o, em, ea, ec, zm, za, zc, ym, ya, yc, pm, p2, pa, pc, q1, qt, qa, lv, tv, zv, yv, zv_sum,
    xs_sem, xr_sem, ks_sem, kr_sem, ds_sem, dr_sem, cs_sem, cr_sem,
    wxs, wxr, wns, wnr, was, war, wfs, wfr, wys, wyr, loc_sem, ps_sem, pr_sem, rs_sem, rr_sem, out_sem,
    zs_sem, zr_sem, as_sem, ar_sem, hs_sem, hr_sem, ys_sem, yr_sem, vs_sem, vr_sem, us_sem, ur_sem,
):
    sec = lax.axis_index("section")
    me = lax.axis_index("shard")
    rep = lax.axis_index("replica")
    x = me // 2
    c = me % 2
    mate = {"shard": x * 2 + 1 - c}
    other = {"section": 1 - sec}
    across_to = {"section": 1 - sec, "replica": flip(rep)}
    kinds = piece_kinds()

    def peer(d):
        return lax.rem(x + d, CHIPS)

    def at_peer(d):
        return {"shard": peer(d) * 2 + c}

    def at_rep(j):
        return {"replica": lax.rem(rep + j, REPL)}

    def at_shard(j):
        return {"shard": lax.rem(me + j, 8)}

    barrier = pltpu.get_barrier_semaphore()
    for j in range(1, REPL):
        pl.semaphore_signal(barrier, inc=1, device_id=at_shard(j), device_id_type=MESH)
        pl.semaphore_signal(barrier, inc=1, device_id=at_rep(j), device_id_type=MESH)
    for where in (other, across_to):
        pl.semaphore_signal(barrier, inc=1, device_id=where, device_id_type=MESH)
    pl.semaphore_wait(barrier, 16)

    def rows_of(chip):
        return pl.ds(pl.multiple_of(chip * ROWS, 32), ROWS)

    def w_src(kind, chip):
        if kind == 0:
            return vec_s
        if kind in (1, 5, 6):
            return wq_s.at[:, pl.ds(pl.multiple_of(QKV[kind] * D + chip * WO, WO), WO)]
        if kind == 2:
            return w1_s.at[:, pl.ds(pl.multiple_of(chip * W1, W1), W1)]
        return wo_s if kind == 3 else w2_s

    def w_dst(layer, kind, chip, core):
        if kind == 0:
            return vecs.at[layer, chip * 2 + core]
        if kind in (1, 2, 5, 6):
            rows = pl.ds(pl.multiple_of((chip * 2 + core) * 128, 128), 128)
            if kind == 2:
                return w1.at[layer, rows]
            return wq.at[layer, rows, pl.ds(QKV[kind] * WO, WO)]
        if kind == 3:
            return wo.at[layer, pl.ds(pl.multiple_of(core * 128, 128), 128)]
        return w2.at[layer, pl.ds(pl.multiple_of(core * 512, 512), 512)]

    def x_copy(kind, d, owner):
        return copy_to(
            w_src(kind, peer(d)), w_dst(sec, kind, owner, c), wxs.at[kind, d], wxr.at[kind, d], at_peer(d)
        )

    def own_piece(kind, d):
        return w_src(kind, x) if d == 0 else w_dst(sec, kind, peer(4 - d), c)

    def near_copy(kind, d, core):
        dst = w_dst(sec, kind, peer(4 - d), core)
        return copy_to(own_piece(kind, d), dst, wns.at[kind, d], wnr.at[kind, d], mate)

    yi = lax.rem(rep, 2)
    y_mate = {"replica": flip(rep)}

    def half_src(kind, h):
        if kind == 0:
            return vec_s
        size = 256 if kind == 4 else 64
        rows = pl.ds(pl.multiple_of(h * size, size), size)
        if kind in QKV:
            return wq_s.at[rows, pl.ds(pl.multiple_of(QKV[kind] * D + x * WO, WO), WO)]
        if kind == 2:
            return w1_s.at[rows, pl.ds(pl.multiple_of(x * W1, W1), W1)]
        return (wo_s if kind == 3 else w2_s).at[rows]

    def half_dst(layer, kind, d, h):
        chip = peer(4 - d)
        if kind == 0:
            return w_dst(layer, kind, chip, c)
        size = 256 if kind == 4 else 64
        base = c if kind in (3, 4) else chip * 2 + c
        rows = pl.ds(pl.multiple_of((base * 2 + h) * size, size), size)
        if kind in QKV:
            return wq.at[layer, rows, pl.ds(QKV[kind] * WO, WO)]
        return {2: w1, 3: wo, 4: w2}[kind].at[layer, rows]

    def across_copy(kind, d, layer, h):
        src = half_src(kind, h) if d == 0 else half_dst(sec, kind, d, h)
        return copy_to(src, half_dst(layer, kind, d, h), was.at[kind, d], war.at[kind, d], across_to)

    def pass_copy(kind, d, h):
        ref = half_dst(1 - sec, kind, d, h)
        return copy_to(ref, ref, wys.at[kind, d], wyr.at[kind, d], y_mate)

    def far_copy(kind, d, core):
        ref = w_dst(1 - sec, kind, peer(4 - d), core)
        return copy_to(ref, ref, wfs.at[kind, d], wfr.at[kind, d], mate)

    def local_copy(kind):
        return pltpu.make_async_copy(w_src(kind, x), w_dst(sec, kind, x, c), loc_sem.at[kind])

    def launch(kind):
        if kind not in (3, 4):
            for d in (1, 3, 2):
                x_copy(kind, d, x).start()
        near_copy(kind, 0, c).start()
        across_copy(kind, 0, sec, yi).start()
        local_copy(kind).start()

    def settle_near(kind):
        for d in kinds[kind][1:]:
            x_copy(kind, d, peer(4 - d)).wait_recv()
            near_copy(kind, d, c).start()
            across_copy(kind, d, sec, yi).start()
        local_copy(kind).wait()
        for d in kinds[kind]:
            near_copy(kind, d, 1 - c).wait_recv()

    def far_in(kind):
        for d in kinds[kind]:
            across_copy(kind, d, 1 - sec, 1 - yi).wait_recv()
            if kind != 0:
                pass_copy(kind, d, 1 - yi).start()

    def far_on(kind):
        for d in kinds[kind]:
            if kind != 0:
                pass_copy(kind, d, yi).wait_recv()
            far_copy(kind, d, c).start()

    def far_done(kind):
        for d in kinds[kind]:
            far_copy(kind, d, 1 - c).wait_recv()

    swap_copy = copy_to(bnd.at[1 - sec], swap, cs_sem.at[0], cr_sem.at[0], other)
    carry_copy = copy_to(carry_s, carry_r, cs_sem.at[1], cr_sem.at[1], other)

    at = 0
    for v in (v_ln1g, v_ln1b, v_qv, v_out, v_ln2g, v_ln2b, v_fc1, v_fc2):
        for t in range(v.shape[1] // 128):
            vec_s[at : at + 1, :] = v[:, t * 128 : t * 128 + 128].astype(F32)
            at += 1
    launch(0)
    swap_copy.start()
    for kind in QKV:
        launch(kind)
    idc[...] = jnp.transpose(jnp.broadcast_to(idr[:1, :], (128, KEYS)))
    settle_near(0)

    @pl.when(sec == 0)
    def _():
        rin[0] = bnd[0].astype(F32)

    @pl.when(sec == 1)
    def _():
        far_in(0)
        far_on(0)
        far_done(0)
        swap_copy.wait_recv()
        rin[0] = swap[...].astype(F32)
        gnext[...] = bnd[1].astype(F32)

    def vec_row(l, k):
        return jnp.concatenate([vecs[l, i, k : k + 1, :] for i in range(8)], axis=1)

    def pieces(l, i, ks):
        part = vecs[l, i]
        return [part[k : k + 1, :] for k in ks]

    def gather_copy(buf, kind, l, d, owner):
        ref = buf.at[l, rows_of(owner)]
        return copy_to(ref, ref, xs_sem.at[kind, l, d], xr_sem.at[kind, l, d], at_peer(d))

    def scatter_copy(kind, l, d):
        return copy_to(
            stage.at[d - 1],
            landed.at[kind // 2, d - 1],
            xs_sem.at[kind, l, d],
            xr_sem.at[kind, l, d],
            at_peer(d),
        )

    def gather_start(buf, kind, l):
        for d in (1, 3, 2):
            gather_copy(buf, kind, l, d, x).start()

    def gather_wait(buf, kind, l, d):
        gather_copy(buf, kind, l, d, peer(4 - d)).wait_recv()

    def scatter_add(kind, l, base):
        total = base
        for d in (1, 3, 2):
            scatter_copy(kind, l, d).wait_recv()
            total = total + landed[kind // 2, d - 1].astype(F32)
        for d in (1, 3, 2):
            scatter_copy(kind, l, d).wait_send()
        return total

    def send_part(kind, l, d, part):
        @pl.when(d == 0)
        def _():
            own[...] = part

        @pl.when(d != 0)
        def _():
            stage[d - 1] = part.astype(BF16)
            scatter_copy(kind, l, d).start()

    def kv_copy(l, d):
        rows = rows_of(peer(4 - d))
        return copy_to(
            qkv.at[l, rows, pl.ds(WO, 2 * WO)], kvp.at[l, rows], ks_sem.at[l, d], kr_sem.at[l, d], mate
        )

    lane = lax.broadcasted_iota(jnp.int32, (1, 128), 1)

    def forward(l, first):
        lower = (l == 0) & (sec == 0)
        upper = (l == 0) & (sec == 1)
        qkv_b = jnp.concatenate(
            pieces(l, x, (2, 3)) + [jnp.zeros((1, WO), F32)] + pieces(l, 4 + x, (2, 3)), axis=1
        )
        fc1_b = jnp.concatenate(
            pieces(l, 2 * x, (7, 8, 9, 10)) + pieces(l, 2 * x + 1, (7, 8, 9, 10)), axis=1
        )
        normed, _ = norm_parts(rin[l])
        n1[l, rows_of(x)] = (normed * vec_row(l, 0) + vec_row(l, 1)).astype(BF16)
        gather_start(n1, AG1, l)

        @pl.when(l == 0)
        def _():
            for kind in QKV:
                settle_near(kind)
            launch(3)
            launch(2)
            launch(4)

        @pl.when(upper)
        def _():
            for step in (far_in, far_on, far_done):
                for kind in QKV:
                    step(kind)

        def project(k, _):
            d = gray(k)
            rows = rows_of(peer(4 - d))

            @pl.when(d != 0)
            def _():
                gather_wait(n1, AG1, l, d)

            qkv[l, rows] = (mm(n1[l, rows], wq[l]) + qkv_b).astype(BF16)
            kv_copy(l, d).start()
            return 0

        lax.fori_loop(0, CHIPS, project, 0)

        @pl.when(l == 0)
        def _():
            settle_near(3)

        @pl.when(upper)
        def _():
            far_in(3)
            far_on(3)
            far_done(3)

        for d in range(CHIPS):
            kv_copy(l, d).wait_recv()

        def attend(j, _):
            d = gray(lax.rem(j + 1, CHIPS))
            rows = rows_of(peer(d))
            bias = jnp.where(idc[rows][:, :1] == idr[:1, :], 0.0, NEG)
            for pair in range(2):
                lanes = slice(pair * 128, pair * 128 + 128)
                q = qkv[l, rows, lanes] * jnp.asarray(HEAD**-0.5, BF16)
                k_own = qkv[l, :, WO + pair * 128 : WO + pair * 128 + 128]
                v_own = qkv[l, :, 2 * WO + pair * 128 : 2 * WO + pair * 128 + 128]
                k_par = kvp[l, :, lanes]
                v_par = kvp[l, :, WO + pair * 128 : WO + pair * 128 + 128]
                low_q = jnp.where(lane < HEAD, q, jnp.zeros_like(q))
                qs = jnp.concatenate([low_q, jnp.where(lane < HEAD, jnp.zeros_like(q), q)], axis=0)
                s = jnp.concatenate([mm_t(qs, k_own), mm_t(qs, k_par)], axis=1)
                s = s.reshape(2, ROWS, KEYS) + bias[None]
                p = jnp.exp(s - jnp.max(s, axis=2, keepdims=True))
                scale = (1.0 / jnp.sum(p, axis=2, keepdims=True)).reshape(2 * ROWS, 1)
                p = p.reshape(2 * ROWS, KEYS).astype(BF16)
                out = (mm(p[:, :TOK], v_own) + mm(p[:, TOK:], v_par)) * scale
                wt[l, rows, lanes] = jnp.where(lane < HEAD, out[:ROWS], out[ROWS:]).astype(BF16)
            send_part(RS1, l, d, mm(wt[l, rows], wo[l]))
            return 0

        lax.fori_loop(0, CHIPS, attend, 0)

        @pl.when(l == 0)
        def _():
            settle_near(2)

        @pl.when(upper)
        def _():
            far_in(2)
            far_in(4)

        rmid[l] = rin[l] + (scatter_add(RS1, l, own[...]) + vec_row(l, 4))
        normed, _ = norm_parts(rmid[l])
        n2[l, rows_of(x)] = (normed * vec_row(l, 5) + vec_row(l, 6)).astype(BF16)
        gather_start(n2, AG2, l)

        @pl.when(l == 0)
        def _():
            settle_near(4)

        @pl.when(upper)
        def _():
            for step in (far_on, far_done):
                step(2)
                step(4)

        @pl.when(lower)
        def _():
            swap_copy.wait_recv()
            gnext[...] = swap[...].astype(F32)
            for kind in (0, 1, 5, 6, 3, 2, 4):
                far_in(kind)

        def feed(k, _):
            d = gray(k)
            back = lax.rem(4 - d, CHIPS)
            rows = rows_of(peer(back))

            @pl.when(d != 0)
            def _():
                gather_wait(n2, AG2, l, d)

            h = mm(n2[l, rows], w1[l]) + fc1_b
            phi = 0.5 + 0.5 * lax.erf(h * (0.5**0.5))
            act[l, rows] = (h * phi).astype(BF16)
            dgl[l, rows] = phi + h * (jnp.exp(-0.5 * h * h) * 0.3989422804014327)
            send_part(RS2, l, back, mm(act[l, rows], w2[l]))
            return 0

        lax.fori_loop(0, CHIPS, feed, 0)

        @pl.when(lower)
        def _():
            for step in (far_on, far_done):
                for kind in (0, 1, 5, 6, 3, 2, 4):
                    step(kind)

        out = rmid[l] + (scatter_add(RS2, l, own[...]) + vec_row(l, 11))

        @pl.when(l == 0)
        def _():
            rin[1] = out.astype(BF16).astype(F32)

        @pl.when((l == 1) & (sec == 0))
        def _():
            carry_s[...] = out.astype(BF16)
            carry_copy.start()

        @pl.when((l == 1) & (sec == 1))
        def _():
            edge_o[1] = out

        return first

    lax.fori_loop(0, 2, forward, 0)

    vg_o[...] = jnp.zeros_like(vg_o)

    def col_sum(v):
        return jnp.sum(v, axis=0, keepdims=True)

    def dkv_copy(l):
        return copy_to(dkv_s.at[l], dkv_r.at[l], ds_sem.at[l], dr_sem.at[l], mate)

    def grads_mlp(l):
        def block(t, _):
            cols = pl.ds(pl.multiple_of(t * 256, 256), 256)
            pgb[t] = over_rows(n2[l, :, cols], dh[l]).astype(BF16).reshape(2, 128, W1)
            half = pl.ds(pl.multiple_of(lax.rem(t, 2) * 256, 256), 256)
            pgd[t // 2, half] = over_rows(act[l, :, cols], g[l]).astype(BF16)
            return 0

        lax.fori_loop(0, CHIPS, block, 0)

    def grads_att(l):
        def block(t, _):
            cols = pl.ds(pl.multiple_of(t * 256, 256), 256)
            pga[t] = over_rows(n1[l, :, cols], dp[l]).astype(BF16).reshape(2, 128, WQ)
            return 0

        lax.fori_loop(0, CHIPS, block, 0)
        pgc[...] = over_rows(wt[l], ga[l]).astype(BF16).reshape(2, 128, D)

    def pair_mlp(l):
        return (
            copy_to(pgb.at[:, 1 - c], rgb, ps_sem.at[l, 1], pr_sem.at[l, 1], mate),
            copy_to(pgd.at[1 - c], rgd, ps_sem.at[l, 3], pr_sem.at[l, 3], mate),
        )

    def pair_att(l):
        return (
            copy_to(pga.at[:, 1 - c], rga, ps_sem.at[l, 0], pr_sem.at[l, 0], mate),
            copy_to(pgc.at[1 - c], rgc, ps_sem.at[l, 2], pr_sem.at[l, 2], mate),
        )

    def piece_of(l, r):
        return r + (l + sec - 2 * l * sec) * (1 - 2 * lax.rem(r, 2))

    def few(p):
        return pl.ds(pl.multiple_of(p * 16, 16), 16)

    def more(p):
        return pl.ds(pl.multiple_of(p * 64, 64), 64)

    def spread_copy(l, n, j):
        p = piece_of(l, lax.rem(rep + j, REPL))
        src = (rga.at[:, few(p)], rgb.at[:, few(p)], rgc.at[few(p)], rgd.at[more(p)])[n]
        return copy_to(src, (lga, lgb, lgc, lgd)[n].at[l, j], rs_sem.at[l, n, j], rr_sem.at[l, n, j], at_rep(j))

    def each_piece(l, ns, act_on):
        def one(j, _):
            for n in ns:
                act_on(spread_copy(l, n, j))
            return 0

        lax.fori_loop(1, REPL, one, 0)

    def sent(cp):
        cp.wait_send()

    def arrived(cp):
        cp.wait_recv()

    def begin(cp):
        cp.start()

    def both(u, v):
        return (u.astype(F32) + v.astype(F32)).astype(BF16)

    def spread_mlp(l):
        for cp in pair_mlp(l):
            cp.wait_recv()
        for t in range(CHIPS):
            rgb[t] = both(pgb[t, c], rgb[t])
        rgd[...] = both(pgd[c], rgd[...])
        p = piece_of(l, rep)
        for t in range(CHIPS):
            em[l, t * 16 : t * 16 + 16] = rgb[t, few(p)].astype(F32)
        em[l, 64:] = rgd[more(p)].astype(F32)
        each_piece(l, (1, 3), begin)

    def spread_att(l):
        for cp in pair_att(l):
            cp.wait_recv()
        for t in range(CHIPS):
            rga[t] = both(pga[t, c], rga[t])
        rgc[...] = both(pgc[c], rgc[...])
        p = piece_of(l, rep)
        for t in range(CHIPS):
            ea[l, t * 16 : t * 16 + 16] = rga[t, few(p)].astype(F32)
        ec[l] = rgc[few(p)].astype(F32)
        each_piece(l, (0, 2), begin)

    def collect_mlp(l):
        each_piece(l, (1, 3), arrived)
        for t in range(CHIPS):
            rows = slice(t * 16, t * 16 + 16)
            total = em[l, rows]
            for j in range(1, REPL):
                total = total + lgb[l, j, t].astype(F32)
            em[l, rows] = total
        total = em[l, 64:]
        for j in range(1, REPL):
            total = total + lgd[l, j].astype(F32)
        em[l, 64:] = total

    def collect_att(l):
        each_piece(l, (0, 2), arrived)
        for t in range(CHIPS):
            rows = slice(t * 16, t * 16 + 16)
            total = ea[l, rows]
            for j in range(1, REPL):
                total = total + lga[l, j, t].astype(F32)
            ea[l, rows] = total
        total = ec[l]
        for j in range(1, REPL):
            total = total + lgc[l, j].astype(F32)
        ec[l] = total

    def backward(i, first):
        l = 1 - i

        def add_vec(k, v):
            vg_o[l, k : k + 1, : v.shape[1]] += v

        def norm_back(v, gain, dy, k):
            xhat, rstd = norm_parts(v)
            add_vec(k, col_sum(dy * xhat))
            add_vec(k + 1, col_sum(dy))
            dyg = dy * gain
            return rstd * (
                dyg - jnp.mean(dyg, axis=-1, keepdims=True) - xhat * jnp.mean(dyg * xhat, axis=-1, keepdims=True)
            )

        low = gnext[...].astype(BF16)
        g[l, rows_of(x)] = low
        gather_start(g, BAG1, l)
        add_vec(7, col_sum(low.astype(F32)))

        @pl.when(i == 1)
        def _():
            grads_att(1)
            each_piece(1, (1, 3), sent)
            for cp in pair_att(1):
                cp.start()
            collect_mlp(1)

        def feed(k, _):
            d = gray(k)
            back = lax.rem(4 - d, CHIPS)
            rows = rows_of(peer(back))

            @pl.when(d != 0)
            def _():
                gather_wait(g, BAG1, l, d)

            d_low = (mm_t(g[l, rows], w2[l]) * dgl[l, rows]).astype(BF16)
            dh[l, rows] = d_low
            add_vec(6, col_sum(d_low.astype(F32)))
            send_part(BRS1, l, back, mm_t(d_low, w1[l]))
            return 0

        lax.fori_loop(0, CHIPS, feed, 0)

        @pl.when(i == 1)
        def _():
            spread_att(1)
            for cp in pair_mlp(1):
                cp.wait_send()

        grads_mlp(l)
        for cp in pair_mlp(l):
            cp.start()
        dn2 = scatter_add(BRS1, l, own[...])
        d_mid = gnext[...] + norm_back(rmid[l], vec_row(l, 5), dn2, 4)
        rmid[l] = d_mid
        low = d_mid.astype(BF16)
        ga[l, rows_of(x)] = low
        gather_start(ga, BAG2, l)
        add_vec(3, col_sum(low.astype(F32)))

        def expand(k, _):
            d = gray(k)
            rows = rows_of(peer(4 - d))

            @pl.when(d != 0)
            def _():
                gather_wait(ga, BAG2, l, d)

            dw[rows] = mm_t(ga[l, rows], wo[l]).astype(BF16)
            return 0

        lax.fori_loop(0, CHIPS, expand, 0)
        spread_mlp(l)
        dkv[...] = jnp.zeros_like(dkv)

        def attend(b, _):
            rows = pl.ds(pl.multiple_of(b * 128, 128), 128)
            bias = jnp.where(idc[:, :1] == idr[:, rows][:1, :], 0.0, NEG)
            for pair in range(2):
                lanes = slice(pair * 128, pair * 128 + 128)
                q = qkv[l, rows, lanes] * jnp.asarray(HEAD**-0.5, BF16)
                do = dw[rows, lanes]
                k_all = jnp.concatenate(
                    [qkv[l, :, WO + pair * 128 : WO + pair * 128 + 128], kvp[l, :, lanes]], axis=0
                )
                v_all = jnp.concatenate(
                    [
                        qkv[l, :, 2 * WO + pair * 128 : 2 * WO + pair * 128 + 128],
                        kvp[l, :, WO + pair * 128 : WO + pair * 128 + 128],
                    ],
                    axis=0,
                )
                none = jnp.zeros_like(q)
                qs = jnp.concatenate([jnp.where(lane < HEAD, q, none), jnp.where(lane < HEAD, none, q)], axis=0)
                dos = jnp.concatenate([jnp.where(lane < HEAD, do, none), jnp.where(lane < HEAD, none, do)], axis=0)
                s = mm_t(k_all, qs) + jnp.concatenate([bias, bias], axis=1)
                p = jnp.exp(s - jnp.max(s, axis=0, keepdims=True))
                p = p * (1.0 / jnp.sum(p, axis=0, keepdims=True))
                dpr = mm_t(v_all, dos)
                ds = (p * (dpr - jnp.sum(p * dpr, axis=0, keepdims=True))).astype(BF16)
                dkv[:, lanes] += mm(ds, qs)
                dkv[:, WO + pair * 128 : WO + pair * 128 + 128] += mm(p.astype(BF16), dos)
                dq = over_rows(ds, k_all)
                dq = jnp.where(lane < HEAD, dq[:128], dq[128:]) * (HEAD**-0.5)
                dp[l, rows, lanes] = dq.astype(BF16)
            return 0

        lax.fori_loop(0, TOK // 128, attend, 0)
        dkv_s[l] = dkv[TOK:].astype(BF16)

        @pl.when(i == 1)
        def _():
            collect_att(1)
            each_piece(1, (0, 2), sent)

        dkv_copy(l).start()
        dkv_copy(l).wait_recv()
        dp[l, :, WO:] = (dkv[:TOK] + dkv_r[l].astype(F32)).astype(BF16)
        add_vec(
            2,
            jnp.concatenate(
                [col_sum(dp[l, :, :WO].astype(F32)), col_sum(dp[l, :, 2 * WO :].astype(F32))], axis=1
            ),
        )

        @pl.when(i == 1)
        def _():
            for cp in pair_att(1):
                cp.wait_send()
            grads_att(0)
            for cp in pair_att(0):
                cp.start()

        def shrink(j, _):
            d = gray(lax.rem(j + 1, CHIPS))
            send_part(BRS2, l, d, mm_t(dp[l, rows_of(peer(d))], wq[l]))
            return 0

        lax.fori_loop(0, CHIPS, shrink, 0)

        @pl.when(i == 1)
        def _():
            spread_att(0)

        dn1 = scatter_add(BRS2, l, own[...])
        d_in = rmid[l] + norm_back(rin[l], vec_row(l, 0), dn1, 0)

        @pl.when(i == 0)
        def _():
            gnext[...] = d_in.astype(BF16).astype(F32)

        @pl.when((i == 1) & (sec == 1))
        def _():
            carry_s[...] = d_in.astype(BF16)
            carry_copy.start()

        @pl.when((i == 1) & (sec == 0))
        def _():
            edge_o[0] = d_in

        return first

    lax.fori_loop(0, 2, backward, 0)

    def vec_copy(j):
        return copy_to(vg_o, lv.at[j], vs_sem.at[j], vr_sem.at[j], at_rep(j))

    def vec_share(j, slot):
        return copy_to(tv, fv.at[slot], us_sem.at[j], ur_sem.at[j], at_shard(j))

    def cross_copy(n):
        src, dst = ((zm, ym), (za, ya), (zc, yc), (zv, yv))[n]
        return copy_to(src, dst, zs_sem.at[n], zr_sem.at[n], across_to)

    def turn_refs(n, source):
        if n == 0:
            return pm, q1.at[:, pl.ds(pl.multiple_of(source * W1, W1), W1)]
        return pa, qt.at[few(source)]

    def turn_copy(n, d, source):
        src, dst = turn_refs(n, source)
        return copy_to(src.at[few(peer(d))], dst, as_sem.at[n, d], ar_sem.at[n, d], at_peer(d))

    def turn_start(n):
        for d in (1, 3, 2):
            turn_copy(n, d, x).start()
        src, dst = turn_refs(n, x)
        dst[...] = src[few(x)]

    def turn_wait(n):
        for d in (1, 3, 2):
            turn_copy(n, d, peer(4 - d)).wait_recv()

    zi = rep // 2
    pieces_of = ((q1, f1), (qa, fa), (pc, fc), (p2, f2))

    def slot_ref(n, slot):
        return pieces_of[n][1].at[more(slot) if n == 3 else few(slot)]

    def slot_of(d, y):
        return lax.rem(zi + 4 - d, 4) * 2 + y

    def along_z(n, d, slot):
        src = pieces_of[n][0]
        where = {"replica": lax.rem(zi + d, 4) * 2 + yi}
        return copy_to(src, slot_ref(n, slot), hs_sem.at[n, d], hr_sem.at[n, d], where)

    def along_z_late(n, d, slot):
        ref = slot_ref(n, slot)
        where = {"replica": lax.rem(zi + d, 4) * 2 + yi}
        return copy_to(ref, ref, hs_sem.at[n, 4 + d], hr_sem.at[n, 4 + d], where)

    def along_y(n, d, y):
        dst = slot_ref(n, slot_of(d, y))
        return copy_to(pieces_of[n][0] if d == 0 else dst, dst, ys_sem.at[n, d], yr_sem.at[n, d], y_mate)

    def keep_piece(n):
        return pltpu.make_async_copy(pieces_of[n][0], slot_ref(n, rep), out_sem.at[n])

    def share_start(n):
        along_y(n, 0, yi).start()
        for d in (1, 3, 2):
            along_z(n, d, rep).start()
        keep_piece(n).start()

    def share_on(n):
        if n in (2, 3):
            along_y(n, 0, 1 - yi).wait_recv()
            for d in (1, 3, 2):
                along_z_late(n, d, flip(rep)).start()
            return
        for d in (1, 3, 2):
            along_z(n, d, slot_of(d, yi)).wait_recv()
            along_y(n, d, yi).start()

    for j in range(1, REPL):
        vec_copy(j).start()
    collect_mlp(0)
    zm[...] = em[1 - sec].astype(BF16)
    cross_copy(0).start()
    total = vg_o[...]
    for j in range(1, REPL):
        vec_copy(j).wait_recv()
        total = total + lv[j]
    vg_o_sum = total
    zv[...] = jnp.where(sec == 0, vg_o_sum[1], vg_o_sum[0])
    cross_copy(3).start()
    cross_copy(0).wait_recv()
    pm[...] = (em[sec, :64] + ym[:64].astype(F32)).astype(BF16)
    p2[...] = (em[sec, 64:] + ym[64:].astype(F32)).astype(BF16)
    turn_start(0)
    share_start(3)
    turn_wait(0)
    share_start(0)
    share_on(3)
    collect_att(0)
    za[...] = ea[1 - sec].astype(BF16)
    zc[...] = ec[1 - sec].astype(BF16)
    cross_copy(1).start()
    cross_copy(2).start()
    cross_copy(3).wait_recv()
    tv[...] = jnp.where(sec == 0, vg_o_sum[0], vg_o_sum[1]) + yv[...]
    fv[me] = tv[...]
    for j in range(1, REPL):
        vec_share(j, me).start()
    cross_copy(1).wait_recv()
    cross_copy(2).wait_recv()
    pa[...] = (ea[sec] + ya[...].astype(F32)).astype(BF16)
    pc[...] = (ec[sec] + yc[...].astype(F32)).astype(BF16)
    turn_start(1)
    share_start(2)
    turn_wait(1)
    for t in range(3):
        for chip in range(CHIPS):
            at = t * D + chip * WO
            qa[:, at : at + WO] = qt[chip * 16 : chip * 16 + 16, t * WO : t * WO + WO]
    share_start(1)
    share_on(0)
    share_on(2)
    share_on(1)
    for n in range(4):
        if n in (2, 3):
            for d in (1, 3, 2):
                along_z(n, d, slot_of(d, yi)).wait_recv()
                along_z_late(n, d, slot_of(d, 1 - yi)).wait_recv()
        else:
            for d in range(4):
                along_y(n, d, 1 - yi).wait_recv()
        keep_piece(n).wait()
    for j in range(1, REPL):
        vec_share(j, lax.rem(me + 8 - j, 8)).wait_recv()
    total = fv[0]
    for n in range(1, 8):
        total = total + fv[n]
    zv_sum[...] = total
    mine = pl.ds(pl.multiple_of(me * 128, 128), 128)
    for row, k in ((0, 0), (1, 1), (4, 3), (5, 4), (6, 5), (11, 7)):
        vo[row : row + 1, :] = zv_sum[k : k + 1, mine]
    for row, k, chip, base, t in [(2, 2, lax.rem(me, 4), me // 4 * 256, t) for t in range(2)] + [
        (7, 6, x, c * 512, t) for t in range(4)
    ]:
        cols = pl.ds(pl.multiple_of(base + t * 128, 128), 128)
        vo[row + t : row + t + 1, :] = fv[2 * chip, k : k + 1, cols] + fv[2 * chip + 1, k : k + 1, cols]

    carry_copy.wait_recv()
    edge_o[1 - sec] = carry_r[...].astype(F32)
    carry_copy.wait_send()
    swap_copy.wait_send()
    for kind in kinds:
        for d in kinds[kind]:
            if d != 0:
                x_copy(kind, d, x).wait_send()
            near_copy(kind, d, c).wait_send()
            across_copy(kind, d, sec, yi).wait_send()
            if kind != 0:
                pass_copy(kind, d, 1 - yi).wait_send()
            far_copy(kind, d, c).wait_send()
    for l in range(2):
        for d in (1, 2, 3):
            for buf, kind in ((n1, AG1), (n2, AG2), (g, BAG1), (ga, BAG2)):
                gather_copy(buf, kind, l, d, x).wait_send()
        for d in range(CHIPS):
            kv_copy(l, d).wait_send()
        dkv_copy(l).wait_send()
    each_piece(0, (0, 1, 2, 3), sent)
    for cp in pair_mlp(0) + pair_att(0):
        cp.wait_send()
    for n in range(4):
        cross_copy(n).wait_send()
    for n in range(2):
        for d in (1, 2, 3):
            turn_copy(n, d, x).wait_send()
    for n in range(4):
        for d in (1, 2, 3):
            along_z(n, d, rep).wait_send()
            if n in (2, 3):
                along_z_late(n, d, flip(rep)).wait_send()
        for d in range(1 if n in (2, 3) else 4):
            along_y(n, d, yi).wait_send()
    for j in range(1, REPL):
        vec_copy(j).wait_send()
        vec_share(j, me).wait_send()


def run_step(*operands):
    vm = pl.BlockSpec(memory_space=pltpu.VMEM)
    hbm = pl.BlockSpec(memory_space=pl.ANY)
    sds = jax.ShapeDtypeStruct
    dma = pltpu.SemaphoreType.DMA
    return pl.pallas_call(
        step_kernel,
        out_shape=(
            sds((MICRO, ROWS, D), F32),
            sds((16, 128), F32),
            sds((128, FF), BF16),
            sds((128, 3 * D), BF16),
            sds((128, D), BF16),
            sds((512, D), BF16),
        ),
        in_specs=[vm] * 10 + [hbm] * 4,
        out_specs=(vm, vm, hbm, hbm, hbm, hbm),
        scratch_shapes=[
            pltpu.VMEM((8, 8, D), F32),
            pltpu.VMEM((KEYS, 128), jnp.int32),
            pltpu.VMEM((16, 128), F32),
            pltpu.VMEM((2, 8, 16, 128), F32),
            pltpu.VMEM((2, D, WQ), BF16),
            pltpu.VMEM((2, WO, D), BF16),
            pltpu.VMEM((2, D, W1), BF16),
            pltpu.VMEM((2, W1, D), BF16),
            pltpu.VMEM((2, TOK, D), BF16),
            pltpu.VMEM((2, TOK, D), BF16),
            pltpu.VMEM((2, TOK, W1), BF16),
            pltpu.VMEM((2, TOK, W1), F32),
            pltpu.VMEM((2, TOK, WQ), BF16),
            pltpu.VMEM((2, TOK, 2 * WO), BF16),
            pltpu.VMEM((2, TOK, WO), BF16),
            pltpu.VMEM((2, ROWS, D), F32),
            pltpu.VMEM((2, ROWS, D), F32),
            pltpu.VMEM((2, TOK, D), BF16),
            pltpu.VMEM((2, TOK, D), BF16),
            pltpu.VMEM((2, TOK, W1), BF16),
            pltpu.VMEM((2, TOK, WQ), BF16),
            pltpu.VMEM((TOK, WO), BF16),
            pltpu.VMEM((3, ROWS, D), BF16),
            pltpu.VMEM((4, 3, ROWS, D), BF16),
            pltpu.VMEM((ROWS, D), BF16),
            pltpu.VMEM((ROWS, D), BF16),
            pltpu.VMEM((ROWS, D), BF16),
            pltpu.VMEM((KEYS, 2 * WO), F32),
            pltpu.VMEM((2, TOK, 2 * WO), BF16),
            pltpu.VMEM((2, TOK, 2 * WO), BF16),
            pltpu.VMEM((ROWS, D), F32),
            pltpu.VMEM((ROWS, D), F32),
            pltpu.VMEM((CHIPS, 2, 128, WQ), BF16),
            pltpu.VMEM((CHIPS, 2, 128, W1), BF16),
            pltpu.VMEM((2, 128, D), BF16),
            pltpu.VMEM((2, 512, D), BF16),
            pltpu.VMEM((CHIPS, 128, WQ), BF16),
            pltpu.VMEM((CHIPS, 128, W1), BF16),
            pltpu.VMEM((128, D), BF16),
            pltpu.VMEM((512, D), BF16),
            pltpu.VMEM((2, REPL, CHIPS, 16, WQ), BF16),
            pltpu.VMEM((2, REPL, CHIPS, 16, W1), BF16),
            pltpu.VMEM((2, REPL, 16, D), BF16),
            pltpu.VMEM((2, REPL, 64, D), BF16),
            pltpu.VMEM((2, 8, D), F32),
            pltpu.VMEM((2, 128, D), F32),
            pltpu.VMEM((2, 64, WQ), F32),
            pltpu.VMEM((2, 16, D), F32),
            pltpu.VMEM((128, D), BF16),
            pltpu.VMEM((64, WQ), BF16),
            pltpu.VMEM((16, D), BF16),
            pltpu.VMEM((128, D), BF16),
            pltpu.VMEM((64, WQ), BF16),
            pltpu.VMEM((16, D), BF16),
            pltpu.VMEM((64, D), BF16),
            pltpu.VMEM((64, D), BF16),
            pltpu.VMEM((64, WQ), BF16),
            pltpu.VMEM((16, D), BF16),
            pltpu.VMEM((16, FF), BF16),
            pltpu.VMEM((64, WQ), BF16),
            pltpu.VMEM((16, 3 * D), BF16),
            pltpu.VMEM((REPL, 2, 8, D), F32),
            pltpu.VMEM((8, D), F32),
            pltpu.VMEM((8, D), F32),
            pltpu.VMEM((8, D), F32),
            pltpu.VMEM((8, D), F32),
            dma((8, 2, CHIPS)),
            dma((8, 2, CHIPS)),
            dma((2, CHIPS)),
            dma((2, CHIPS)),
            dma((2,)),
            dma((2,)),
            dma((2,)),
            dma((2,)),
            dma((7, CHIPS)),
            dma((7, CHIPS)),
            dma((7, CHIPS)),
            dma((7, CHIPS)),
            dma((7, CHIPS)),
            dma((7, CHIPS)),
            dma((7, CHIPS)),
            dma((7, CHIPS)),
            dma((7, CHIPS)),
            dma((7, CHIPS)),
            dma((7,)),
            dma((2, 4)),
            dma((2, 4)),
            dma((2, 4, REPL)),
            dma((2, 4, REPL)),
            dma((4,)),
            dma((4,)),
            dma((4,)),
            dma((2, CHIPS)),
            dma((2, CHIPS)),
            dma((4, 8)),
            dma((4, 8)),
            dma((4, 4)),
            dma((4, 4)),
            dma((REPL,)),
            dma((REPL,)),
            dma((REPL,)),
            dma((REPL,)),
        ],
        compiler_params=pltpu.CompilerParams(
            collective_id=0, has_side_effects=True, vmem_limit_bytes=63 * 1024 * 1024
        ),
    )(*operands)


def body(
    boundary, image_of_token, ln1_gain, ln1_bias, w_qkv, qv_bias, w_out, out_bias,
    ln2_gain, ln2_bias, w_fc1, fc1_bias, w_fc2, fc2_bias,
):
    me = lax.axis_index("shard")
    x, c = me // 2, me % 2
    sec = lax.axis_index("section")
    bnd = boundary[0, :, 0]
    ids = lax.dynamic_index_in_dim(image_of_token[:, 0], sec, 0, keepdims=False).reshape(CHIPS, 2, ROWS)
    flipped = jnp.where(c == 0, ids, ids[:, ::-1])
    ids = jnp.swapaxes(flipped, 0, 1).reshape(KEYS)
    idr = jnp.broadcast_to(ids[None, :], (8, KEYS))
    edge, vo, f1, fa, fc, f2 = run_step(
        bnd, idr, ln1_gain, ln1_bias, qv_bias, out_bias, ln2_gain, ln2_bias, fc1_bias, fc2_bias,
        w_qkv[0], w_out[0], w_fc1[0], w_fc2[0],
    )
    g_qkv, g_fc1, g_out, g_fc2 = (v.astype(F32) for v in (fa, f1, fc, f2))

    def part(at, count):
        return vo[at : at + count].reshape(1, count * 128)

    return (
        edge[None, :, None],
        part(0, 1),
        part(1, 1),
        g_qkv[None],
        part(2, 2),
        g_out[None],
        part(4, 1),
        part(5, 1),
        part(6, 1),
        g_fc1[None],
        part(7, 4),
        g_fc2[None],
        part(11, 1),
    )


def solution(mesh):
    row = P("section", "shard")
    mat = P("section", "shard", None)
    edge = P("section", None, "replica", "shard", None)
    in_specs = (edge, P(None, "replica", None), row, row, mat, row, mat, row, row, row, mat, row, mat, row)
    out_specs = (edge, row, row, mat, row, mat, row, row, row, mat, row, mat, row)
    return jax.shard_map(body, mesh=mesh, in_specs=in_specs, out_specs=out_specs, check_vma=False)
```

```python
import functools

import jax
import jax.numpy as jnp
from jax import lax
from jax.experimental import pallas as pl
from jax.experimental.pallas import tpu as pltpu
from jax.sharding import PartitionSpec as P

D = 1024
HEADS = 16
HEAD = 64
FF = 4096
EPS = 1e-06
NEG = -1e30

MICRO = 2
CHIPS = 4
ROWS = 96
TOK = CHIPS * ROWS
KEYS = 2 * TOK
WQ = 3 * D // CHIPS
WO = D // CHIPS
W1 = FF // CHIPS
REPL = 8

MESH = pl.DeviceIdType.MESH
F32 = jnp.float32
BF16 = jnp.bfloat16

AG1, RS1, AG2, RS2, BAG1, BRS1, BAG2, BRS2 = range(8)


def mm(a, b):
    return jnp.dot(a, b, preferred_element_type=F32)


def mm_t(a, b):
    return lax.dot_general(a, b, (((1,), (1,)), ((), ())), preferred_element_type=F32)


def over_rows(a, b):
    return lax.dot_general(a, b, (((0,), (0,)), ((), ())), preferred_element_type=F32)


def norm_parts(v):
    centered = v - jnp.mean(v, axis=-1, keepdims=True)
    rstd = lax.rsqrt(jnp.mean(centered * centered, axis=-1, keepdims=True) + EPS)
    return centered * rstd, rstd


def gray(k):
    return k + k // 2 - 2 * (k // 3)


def flip(r):
    return r + 1 - 2 * lax.rem(r, 2)


def copy_to(src, dst, send, recv, where):
    return pltpu.make_async_remote_copy(
        src_ref=src, dst_ref=dst, send_sem=send, recv_sem=recv, device_id=where, device_id_type=MESH
    )


QKV = {1: 0, 5: 1, 6: 2}


def piece_kinds():
    table = {kind: (0, 1, 3, 2) for kind in (0, 1, 2, 5, 6)}
    table.update({3: (0,), 4: (0,)})
    return table


def step_kernel(
    bnd, idr, v_ln1g, v_ln1b, v_qv, v_out, v_ln2g, v_ln2b, v_fc1, v_fc2, wq_s, wo_s, w1_s, w2_s,
    edge_o, vo, f1, fa, fc, f2,
    fv, idc, vec_s, vecs, wq, wo, w1, w2,
    n1, n2, act, dgl, qkv, kvp, wt, rin, rmid, g, ga, dh, dp, dw,
    stage, landed, swap, carry_s, carry_r, dkv, dkv_s, dkv_r, own, gnext,
    pga, pgb, pgc, pgd, rga, rgb, rgc, rgd, lga, lgb, lgc, lgd,
    vg_o, em, ea, ec, zm, za, zc, ym, ya, yc, pm, p2, pa, pc, q1, qt, qa, lv, tv, zv, yv, zv_sum,
    xs_sem, xr_sem, ks_sem, kr_sem, ds_sem, dr_sem, cs_sem, cr_sem,
    wxs, wxr, wns, wnr, was, war, wfs, wfr, wys, wyr, loc_sem, ps_sem, pr_sem, rs_sem, rr_sem, out_sem,
    zs_sem, zr_sem, as_sem, ar_sem, hs_sem, hr_sem, ys_sem, yr_sem, vs_sem, vr_sem, us_sem, ur_sem,
):
    sec = lax.axis_index("section")
    me = lax.axis_index("shard")
    rep = lax.axis_index("replica")
    x = me // 2
    c = me % 2
    mate = {"shard": x * 2 + 1 - c}
    other = {"section": 1 - sec}
    across_to = {"section": 1 - sec, "replica": flip(rep)}
    kinds = piece_kinds()

    def peer(d):
        return lax.rem(x + d, CHIPS)

    def at_peer(d):
        return {"shard": peer(d) * 2 + c}

    def at_rep(j):
        return {"replica": lax.rem(rep + j, REPL)}

    def at_shard(j):
        return {"shard": lax.rem(me + j, 8)}

    barrier = pltpu.get_barrier_semaphore()
    for j in range(1, REPL):
        pl.semaphore_signal(barrier, inc=1, device_id=at_shard(j), device_id_type=MESH)
        pl.semaphore_signal(barrier, inc=1, device_id=at_rep(j), device_id_type=MESH)
    for where in (other, across_to):
        pl.semaphore_signal(barrier, inc=1, device_id=where, device_id_type=MESH)
    pl.semaphore_wait(barrier, 16)

    def rows_of(chip):
        return pl.ds(pl.multiple_of(chip * ROWS, 32), ROWS)

    def w_src(kind, chip):
        if kind == 0:
            return vec_s
        if kind in (1, 5, 6):
            return wq_s.at[:, pl.ds(pl.multiple_of(QKV[kind] * D + chip * WO, WO), WO)]
        if kind == 2:
            return w1_s.at[:, pl.ds(pl.multiple_of(chip * W1, W1), W1)]
        return wo_s if kind == 3 else w2_s

    def w_dst(layer, kind, chip, core):
        if kind == 0:
            return vecs.at[layer, chip * 2 + core]
        if kind in (1, 2, 5, 6):
            rows = pl.ds(pl.multiple_of((chip * 2 + core) * 128, 128), 128)
            if kind == 2:
                return w1.at[layer, rows]
            return wq.at[layer, rows, pl.ds(QKV[kind] * WO, WO)]
        if kind == 3:
            return wo.at[layer, pl.ds(pl.multiple_of(core * 128, 128), 128)]
        return w2.at[layer, pl.ds(pl.multiple_of(core * 512, 512), 512)]

    def x_copy(kind, d, owner):
        return copy_to(
            w_src(kind, peer(d)), w_dst(sec, kind, owner, c), wxs.at[kind, d], wxr.at[kind, d], at_peer(d)
        )

    def own_piece(kind, d):
        return w_src(kind, x) if d == 0 else w_dst(sec, kind, peer(4 - d), c)

    def near_copy(kind, d, core):
        dst = w_dst(sec, kind, peer(4 - d), core)
        return copy_to(own_piece(kind, d), dst, wns.at[kind, d], wnr.at[kind, d], mate)

    yi = lax.rem(rep, 2)
    y_mate = {"replica": flip(rep)}

    def half_src(kind, h):
        if kind == 0:
            return vec_s
        size = 256 if kind == 4 else 64
        rows = pl.ds(pl.multiple_of(h * size, size), size)
        if kind in QKV:
            return wq_s.at[rows, pl.ds(pl.multiple_of(QKV[kind] * D + x * WO, WO), WO)]
        if kind == 2:
            return w1_s.at[rows, pl.ds(pl.multiple_of(x * W1, W1), W1)]
        return (wo_s if kind == 3 else w2_s).at[rows]

    def half_dst(layer, kind, d, h):
        chip = peer(4 - d)
        if kind == 0:
            return w_dst(layer, kind, chip, c)
        size = 256 if kind == 4 else 64
        base = c if kind in (3, 4) else chip * 2 + c
        rows = pl.ds(pl.multiple_of((base * 2 + h) * size, size), size)
        if kind in QKV:
            return wq.at[layer, rows, pl.ds(QKV[kind] * WO, WO)]
        return {2: w1, 3: wo, 4: w2}[kind].at[layer, rows]

    def across_copy(kind, d, layer, h):
        src = half_src(kind, h) if d == 0 else half_dst(sec, kind, d, h)
        return copy_to(src, half_dst(layer, kind, d, h), was.at[kind, d], war.at[kind, d], across_to)

    def pass_copy(kind, d, h):
        ref = half_dst(1 - sec, kind, d, h)
        return copy_to(ref, ref, wys.at[kind, d], wyr.at[kind, d], y_mate)

    def far_copy(kind, d, core):
        ref = w_dst(1 - sec, kind, peer(4 - d), core)
        return copy_to(ref, ref, wfs.at[kind, d], wfr.at[kind, d], mate)

    def local_copy(kind):
        return pltpu.make_async_copy(w_src(kind, x), w_dst(sec, kind, x, c), loc_sem.at[kind])

    def launch(kind):
        if kind not in (3, 4):
            for d in (1, 3, 2):
                x_copy(kind, d, x).start()
        near_copy(kind, 0, c).start()
        across_copy(kind, 0, sec, yi).start()
        local_copy(kind).start()

    def settle_near(kind):
        for d in kinds[kind][1:]:
            x_copy(kind, d, peer(4 - d)).wait_recv()
            near_copy(kind, d, c).start()
            across_copy(kind, d, sec, yi).start()
        local_copy(kind).wait()
        for d in kinds[kind]:
            near_copy(kind, d, 1 - c).wait_recv()

    def far_in(kind):
        for d in kinds[kind]:
            across_copy(kind, d, 1 - sec, 1 - yi).wait_recv()
            if kind != 0:
                pass_copy(kind, d, 1 - yi).start()

    def far_on(kind):
        for d in kinds[kind]:
            if kind != 0:
                pass_copy(kind, d, yi).wait_recv()
            far_copy(kind, d, c).start()

    def far_done(kind):
        for d in kinds[kind]:
            far_copy(kind, d, 1 - c).wait_recv()

    swap_copy = copy_to(bnd.at[1 - sec], swap, cs_sem.at[0], cr_sem.at[0], other)
    carry_copy = copy_to(carry_s, carry_r, cs_sem.at[1], cr_sem.at[1], other)

    at = 0
    for v in (v_ln1g, v_ln1b, v_qv, v_out, v_ln2g, v_ln2b, v_fc1, v_fc2):
        for t in range(v.shape[1] // 128):
            vec_s[at : at + 1, :] = v[:, t * 128 : t * 128 + 128].astype(F32)
            at += 1
    launch(0)
    swap_copy.start()
    for kind in QKV:
        launch(kind)
    idc[...] = jnp.transpose(jnp.broadcast_to(idr[:1, :], (128, KEYS)))
    settle_near(0)

    @pl.when(sec == 0)
    def _():
        rin[0] = bnd[0].astype(F32)

    @pl.when(sec == 1)
    def _():
        far_in(0)
        far_on(0)
        far_done(0)
        swap_copy.wait_recv()
        rin[0] = swap[...].astype(F32)
        gnext[...] = bnd[1].astype(F32)

    def vec_row(l, k):
        return jnp.concatenate([vecs[l, i, k : k + 1, :] for i in range(8)], axis=1)

    def pieces(l, i, ks):
        part = vecs[l, i]
        return [part[k : k + 1, :] for k in ks]

    def gather_copy(buf, kind, l, d, owner):
        ref = buf.at[l, rows_of(owner)]
        return copy_to(ref, ref, xs_sem.at[kind, l, d], xr_sem.at[kind, l, d], at_peer(d))

    def scatter_copy(kind, l, d):
        return copy_to(
            stage.at[d - 1],
            landed.at[kind // 2, d - 1],
            xs_sem.at[kind, l, d],
            xr_sem.at[kind, l, d],
            at_peer(d),
        )

    def gather_start(buf, kind, l):
        for d in (1, 3, 2):
            gather_copy(buf, kind, l, d, x).start()

    def gather_wait(buf, kind, l, d):
        gather_copy(buf, kind, l, d, peer(4 - d)).wait_recv()

    def scatter_add(kind, l, base):
        total = base
        for d in (1, 3, 2):
            scatter_copy(kind, l, d).wait_recv()
            total = total + landed[kind // 2, d - 1].astype(F32)
        for d in (1, 3, 2):
            scatter_copy(kind, l, d).wait_send()
        return total

    def send_part(kind, l, d, part):
        @pl.when(d == 0)
        def _():
            own[...] = part

        @pl.when(d != 0)
        def _():
            stage[d - 1] = part.astype(BF16)
            scatter_copy(kind, l, d).start()

    def kv_copy(l, d):
        rows = rows_of(peer(4 - d))
        return copy_to(
            qkv.at[l, rows, pl.ds(WO, 2 * WO)], kvp.at[l, rows], ks_sem.at[l, d], kr_sem.at[l, d], mate
        )

    lane = lax.broadcasted_iota(jnp.int32, (1, 128), 1)

    def forward(l, first):
        lower = (l == 0) & (sec == 0)
        upper = (l == 0) & (sec == 1)
        qkv_b = jnp.concatenate(
            pieces(l, x, (2, 3)) + [jnp.zeros((1, WO), F32)] + pieces(l, 4 + x, (2, 3)), axis=1
        )
        fc1_b = jnp.concatenate(
            pieces(l, 2 * x, (7, 8, 9, 10)) + pieces(l, 2 * x + 1, (7, 8, 9, 10)), axis=1
        )
        normed, _ = norm_parts(rin[l])
        n1[l, rows_of(x)] = (normed * vec_row(l, 0) + vec_row(l, 1)).astype(BF16)
        gather_start(n1, AG1, l)

        @pl.when(l == 0)
        def _():
            for kind in QKV:
                settle_near(kind)
            launch(3)
            launch(2)
            launch(4)

        @pl.when(upper)
        def _():
            for step in (far_in, far_on, far_done):
                for kind in QKV:
                    step(kind)

        def project(k, _):
            d = gray(k)
            rows = rows_of(peer(4 - d))

            @pl.when(d != 0)
            def _():
                gather_wait(n1, AG1, l, d)

            qkv[l, rows] = (mm(n1[l, rows], wq[l]) + qkv_b).astype(BF16)
            kv_copy(l, d).start()
            return 0

        lax.fori_loop(0, CHIPS, project, 0)

        @pl.when(l == 0)
        def _():
            settle_near(3)

        @pl.when(upper)
        def _():
            far_in(3)
            far_on(3)
            far_done(3)

        for d in range(CHIPS):
            kv_copy(l, d).wait_recv()

        def attend(j, _):
            d = gray(lax.rem(j + 1, CHIPS))
            rows = rows_of(peer(d))
            bias = jnp.where(idc[rows][:, :1] == idr[:1, :], 0.0, NEG)
            for pair in range(2):
                lanes = slice(pair * 128, pair * 128 + 128)
                q = qkv[l, rows, lanes] * jnp.asarray(HEAD**-0.5, BF16)
                k_own = qkv[l, :, WO + pair * 128 : WO + pair * 128 + 128]
                v_own = qkv[l, :, 2 * WO + pair * 128 : 2 * WO + pair * 128 + 128]
                k_par = kvp[l, :, lanes]
                v_par = kvp[l, :, WO + pair * 128 : WO + pair * 128 + 128]
                low_q = jnp.where(lane < HEAD, q, jnp.zeros_like(q))
                qs = jnp.concatenate([low_q, jnp.where(lane < HEAD, jnp.zeros_like(q), q)], axis=0)
                s = jnp.concatenate([mm_t(qs, k_own), mm_t(qs, k_par)], axis=1)
                s = s.reshape(2, ROWS, KEYS) + bias[None]
                p = jnp.exp(s - jnp.max(s, axis=2, keepdims=True))
                scale = (1.0 / jnp.sum(p, axis=2, keepdims=True)).reshape(2 * ROWS, 1)
                p = p.reshape(2 * ROWS, KEYS).astype(BF16)
                out = (mm(p[:, :TOK], v_own) + mm(p[:, TOK:], v_par)) * scale
                wt[l, rows, lanes] = jnp.where(lane < HEAD, out[:ROWS], out[ROWS:]).astype(BF16)
            send_part(RS1, l, d, mm(wt[l, rows], wo[l]))
            return 0

        lax.fori_loop(0, CHIPS, attend, 0)

        @pl.when(l == 0)
        def _():
            settle_near(2)

        @pl.when(upper)
        def _():
            far_in(2)
            far_in(4)

        rmid[l] = rin[l] + (scatter_add(RS1, l, own[...]) + vec_row(l, 4))
        normed, _ = norm_parts(rmid[l])
        n2[l, rows_of(x)] = (normed * vec_row(l, 5) + vec_row(l, 6)).astype(BF16)
        gather_start(n2, AG2, l)

        @pl.when(l == 0)
        def _():
            settle_near(4)

        @pl.when(upper)
        def _():
            for step in (far_on, far_done):
                step(2)
                step(4)

        @pl.when(lower)
        def _():
            swap_copy.wait_recv()
            gnext[...] = swap[...].astype(F32)
            for kind in (0, 1, 5, 6, 3, 2, 4):
                far_in(kind)

        def feed(k, _):
            d = gray(k)
            back = lax.rem(4 - d, CHIPS)
            rows = rows_of(peer(back))

            @pl.when(d != 0)
            def _():
                gather_wait(n2, AG2, l, d)

            h = mm(n2[l, rows], w1[l]) + fc1_b
            phi = 0.5 + 0.5 * lax.erf(h * (0.5**0.5))
            act[l, rows] = (h * phi).astype(BF16)
            dgl[l, rows] = phi + h * (jnp.exp(-0.5 * h * h) * 0.3989422804014327)
            send_part(RS2, l, back, mm(act[l, rows], w2[l]))
            return 0

        lax.fori_loop(0, CHIPS, feed, 0)

        @pl.when(lower)
        def _():
            for step in (far_on, far_done):
                for kind in (0, 1, 5, 6, 3, 2, 4):
                    step(kind)

        out = rmid[l] + (scatter_add(RS2, l, own[...]) + vec_row(l, 11))

        @pl.when(l == 0)
        def _():
            rin[1] = out.astype(BF16).astype(F32)

        @pl.when((l == 1) & (sec == 0))
        def _():
            carry_s[...] = out.astype(BF16)
            carry_copy.start()

        @pl.when((l == 1) & (sec == 1))
        def _():
            edge_o[1] = out

        return first

    lax.fori_loop(0, 2, forward, 0)

    vg_o[...] = jnp.zeros_like(vg_o)

    def col_sum(v):
        return jnp.sum(v, axis=0, keepdims=True)

    def dkv_copy(l):
        return copy_to(dkv_s.at[l], dkv_r.at[l], ds_sem.at[l], dr_sem.at[l], mate)

    def grads_mlp(l):
        def block(t, _):
            cols = pl.ds(pl.multiple_of(t * 256, 256), 256)
            pgb[t] = over_rows(n2[l, :, cols], dh[l]).astype(BF16).reshape(2, 128, W1)
            half = pl.ds(pl.multiple_of(lax.rem(t, 2) * 256, 256), 256)
            pgd[t // 2, half] = over_rows(act[l, :, cols], g[l]).astype(BF16)
            return 0

        lax.fori_loop(0, CHIPS, block, 0)

    def grads_att(l):
        def block(t, _):
            cols = pl.ds(pl.multiple_of(t * 256, 256), 256)
            pga[t] = over_rows(n1[l, :, cols], dp[l]).astype(BF16).reshape(2, 128, WQ)
            return 0

        lax.fori_loop(0, CHIPS, block, 0)
        pgc[...] = over_rows(wt[l], ga[l]).astype(BF16).reshape(2, 128, D)

    def pair_mlp(l):
        return (
            copy_to(pgb.at[:, 1 - c], rgb, ps_sem.at[l, 1], pr_sem.at[l, 1], mate),
            copy_to(pgd.at[1 - c], rgd, ps_sem.at[l, 3], pr_sem.at[l, 3], mate),
        )

    def pair_att(l):
        return (
            copy_to(pga.at[:, 1 - c], rga, ps_sem.at[l, 0], pr_sem.at[l, 0], mate),
            copy_to(pgc.at[1 - c], rgc, ps_sem.at[l, 2], pr_sem.at[l, 2], mate),
        )

    def piece_of(l, r):
        return r + (l + sec - 2 * l * sec) * (1 - 2 * lax.rem(r, 2))

    def few(p):
        return pl.ds(pl.multiple_of(p * 16, 16), 16)

    def more(p):
        return pl.ds(pl.multiple_of(p * 64, 64), 64)

    def spread_copy(l, n, j):
        p = piece_of(l, lax.rem(rep + j, REPL))
        src = (rga.at[:, few(p)], rgb.at[:, few(p)], rgc.at[few(p)], rgd.at[more(p)])[n]
        return copy_to(src, (lga, lgb, lgc, lgd)[n].at[l, j], rs_sem.at[l, n, j], rr_sem.at[l, n, j], at_rep(j))

    def each_piece(l, ns, act_on):
        def one(j, _):
            for n in ns:
                act_on(spread_copy(l, n, j))
            return 0

        lax.fori_loop(1, REPL, one, 0)

    def sent(cp):
        cp.wait_send()

    def arrived(cp):
        cp.wait_recv()

    def begin(cp):
        cp.start()

    def both(u, v):
        return (u.astype(F32) + v.astype(F32)).astype(BF16)

    def spread_mlp(l):
        for cp in pair_mlp(l):
            cp.wait_recv()
        for t in range(CHIPS):
            rgb[t] = both(pgb[t, c], rgb[t])
        rgd[...] = both(pgd[c], rgd[...])
        p = piece_of(l, rep)
        for t in range(CHIPS):
            em[l, t * 16 : t * 16 + 16] = rgb[t, few(p)].astype(F32)
        em[l, 64:] = rgd[more(p)].astype(F32)
        each_piece(l, (1, 3), begin)

    def spread_att(l):
        for cp in pair_att(l):
            cp.wait_recv()
        for t in range(CHIPS):
            rga[t] = both(pga[t, c], rga[t])
        rgc[...] = both(pgc[c], rgc[...])
        p = piece_of(l, rep)
        for t in range(CHIPS):
            ea[l, t * 16 : t * 16 + 16] = rga[t, few(p)].astype(F32)
        ec[l] = rgc[few(p)].astype(F32)
        each_piece(l, (0, 2), begin)

    def collect_mlp(l):
        each_piece(l, (1, 3), arrived)
        for t in range(CHIPS):
            rows = slice(t * 16, t * 16 + 16)
            total = em[l, rows]
            for j in range(1, REPL):
                total = total + lgb[l, j, t].astype(F32)
            em[l, rows] = total
        total = em[l, 64:]
        for j in range(1, REPL):
            total = total + lgd[l, j].astype(F32)
        em[l, 64:] = total

    def collect_att(l):
        each_piece(l, (0, 2), arrived)
        for t in range(CHIPS):
            rows = slice(t * 16, t * 16 + 16)
            total = ea[l, rows]
            for j in range(1, REPL):
                total = total + lga[l, j, t].astype(F32)
            ea[l, rows] = total
        total = ec[l]
        for j in range(1, REPL):
            total = total + lgc[l, j].astype(F32)
        ec[l] = total

    def cross_copy(n):
        src, dst = ((zm, ym), (za, ya), (zc, yc), (zv, yv))[n]
        return copy_to(src, dst, zs_sem.at[n], zr_sem.at[n], across_to)

    def backward(i, first):
        l = 1 - i

        def add_vec(k, v):
            vg_o[l, k : k + 1, : v.shape[1]] += v

        def norm_back(v, gain, dy, k):
            xhat, rstd = norm_parts(v)
            add_vec(k, col_sum(dy * xhat))
            add_vec(k + 1, col_sum(dy))
            dyg = dy * gain
            return rstd * (
                dyg - jnp.mean(dyg, axis=-1, keepdims=True) - xhat * jnp.mean(dyg * xhat, axis=-1, keepdims=True)
            )

        low = gnext[...].astype(BF16)
        g[l, rows_of(x)] = low
        gather_start(g, BAG1, l)
        add_vec(7, col_sum(low.astype(F32)))

        @pl.when(i == 1)
        def _():
            grads_att(1)
            each_piece(1, (1, 3), sent)
            for cp in pair_att(1):
                cp.start()
            collect_mlp(1)

        def feed(k, _):
            d = gray(k)
            back = lax.rem(4 - d, CHIPS)
            rows = rows_of(peer(back))

            @pl.when(d != 0)
            def _():
                gather_wait(g, BAG1, l, d)

            d_low = (mm_t(g[l, rows], w2[l]) * dgl[l, rows]).astype(BF16)
            dh[l, rows] = d_low
            add_vec(6, col_sum(d_low.astype(F32)))
            send_part(BRS1, l, back, mm_t(d_low, w1[l]))
            return 0

        lax.fori_loop(0, CHIPS, feed, 0)

        @pl.when(i == 1)
        def _():
            spread_att(1)
            for cp in pair_mlp(1):
                cp.wait_send()

        grads_mlp(l)
        for cp in pair_mlp(l):
            cp.start()
        dn2 = scatter_add(BRS1, l, own[...])
        d_mid = gnext[...] + norm_back(rmid[l], vec_row(l, 5), dn2, 4)
        rmid[l] = d_mid
        low = d_mid.astype(BF16)
        ga[l, rows_of(x)] = low
        gather_start(ga, BAG2, l)
        add_vec(3, col_sum(low.astype(F32)))

        def expand(k, _):
            d = gray(k)
            rows = rows_of(peer(4 - d))

            @pl.when(d != 0)
            def _():
                gather_wait(ga, BAG2, l, d)

            dw[rows] = mm_t(ga[l, rows], wo[l]).astype(BF16)
            return 0

        lax.fori_loop(0, CHIPS, expand, 0)
        spread_mlp(l)
        dkv[...] = jnp.zeros_like(dkv)

        def attend(b, _):
            rows = pl.ds(pl.multiple_of(b * 128, 128), 128)
            bias = jnp.where(idc[:, :1] == idr[:, rows][:1, :], 0.0, NEG)
            for pair in range(2):
                lanes = slice(pair * 128, pair * 128 + 128)
                q = qkv[l, rows, lanes] * jnp.asarray(HEAD**-0.5, BF16)
                do = dw[rows, lanes]
                k_all = jnp.concatenate(
                    [qkv[l, :, WO + pair * 128 : WO + pair * 128 + 128], kvp[l, :, lanes]], axis=0
                )
                v_all = jnp.concatenate(
                    [
                        qkv[l, :, 2 * WO + pair * 128 : 2 * WO + pair * 128 + 128],
                        kvp[l, :, WO + pair * 128 : WO + pair * 128 + 128],
                    ],
                    axis=0,
                )
                none = jnp.zeros_like(q)
                qs = jnp.concatenate([jnp.where(lane < HEAD, q, none), jnp.where(lane < HEAD, none, q)], axis=0)
                dos = jnp.concatenate([jnp.where(lane < HEAD, do, none), jnp.where(lane < HEAD, none, do)], axis=0)
                s = mm_t(k_all, qs) + jnp.concatenate([bias, bias], axis=1)
                p = jnp.exp(s - jnp.max(s, axis=0, keepdims=True))
                p = p * (1.0 / jnp.sum(p, axis=0, keepdims=True))
                dpr = mm_t(v_all, dos)
                ds = (p * (dpr - jnp.sum(p * dpr, axis=0, keepdims=True))).astype(BF16)
                dkv[:, lanes] += mm(ds, qs)
                dkv[:, WO + pair * 128 : WO + pair * 128 + 128] += mm(p.astype(BF16), dos)
                dq = over_rows(ds, k_all)
                dq = jnp.where(lane < HEAD, dq[:128], dq[128:]) * (HEAD**-0.5)
                dp[l, rows, lanes] = dq.astype(BF16)
            return 0

        lax.fori_loop(0, TOK // 128, attend, 0)
        dkv_s[l] = dkv[TOK:].astype(BF16)

        @pl.when(i == 1)
        def _():
            collect_att(1)
            each_piece(1, (0, 2), sent)

        dkv_copy(l).start()
        dkv_copy(l).wait_recv()
        dp[l, :, WO:] = (dkv[:TOK] + dkv_r[l].astype(F32)).astype(BF16)
        add_vec(
            2,
            jnp.concatenate(
                [col_sum(dp[l, :, :WO].astype(F32)), col_sum(dp[l, :, 2 * WO :].astype(F32))], axis=1
            ),
        )

        @pl.when(i == 1)
        def _():
            for cp in pair_att(1):
                cp.wait_send()
            grads_att(0)
            for cp in pair_att(0):
                cp.start()

        def shrink(j, _):
            d = gray(lax.rem(j + 1, CHIPS))
            send_part(BRS2, l, d, mm_t(dp[l, rows_of(peer(d))], wq[l]))
            return 0

        lax.fori_loop(0, CHIPS, shrink, 0)

        @pl.when(i == 1)
        def _():
            spread_att(0)
            collect_mlp(0)
            zm[...] = em[1 - sec].astype(BF16)
            cross_copy(0).start()

        dn1 = scatter_add(BRS2, l, own[...])
        d_in = rmid[l] + norm_back(rin[l], vec_row(l, 0), dn1, 0)

        @pl.when(i == 0)
        def _():
            gnext[...] = d_in.astype(BF16).astype(F32)

        @pl.when((i == 1) & (sec == 1))
        def _():
            carry_s[...] = d_in.astype(BF16)
            carry_copy.start()

        @pl.when((i == 1) & (sec == 0))
        def _():
            edge_o[0] = d_in

        return first

    lax.fori_loop(0, 2, backward, 0)

    def vec_copy(j):
        return copy_to(vg_o, lv.at[j], vs_sem.at[j], vr_sem.at[j], at_rep(j))

    def vec_share(j, slot):
        return copy_to(tv, fv.at[slot], us_sem.at[j], ur_sem.at[j], at_shard(j))

    def turn_refs(n, source):
        if n == 0:
            return pm, q1.at[:, pl.ds(pl.multiple_of(source * W1, W1), W1)]
        return pa, qt.at[few(source)]

    def turn_copy(n, d, source):
        src, dst = turn_refs(n, source)
        return copy_to(src.at[few(peer(d))], dst, as_sem.at[n, d], ar_sem.at[n, d], at_peer(d))

    def turn_start(n):
        for d in (1, 3, 2):
            turn_copy(n, d, x).start()
        src, dst = turn_refs(n, x)
        dst[...] = src[few(x)]

    def turn_wait(n):
        for d in (1, 3, 2):
            turn_copy(n, d, peer(4 - d)).wait_recv()

    zi = rep // 2
    pieces_of = ((q1, f1), (qa, fa), (pc, fc), (p2, f2))

    def slot_ref(n, slot):
        return pieces_of[n][1].at[more(slot) if n == 3 else few(slot)]

    def slot_of(d, y):
        return lax.rem(zi + 4 - d, 4) * 2 + y

    def along_z(n, d, slot):
        src = pieces_of[n][0]
        where = {"replica": lax.rem(zi + d, 4) * 2 + yi}
        return copy_to(src, slot_ref(n, slot), hs_sem.at[n, d], hr_sem.at[n, d], where)

    def along_z_late(n, d, slot):
        ref = slot_ref(n, slot)
        where = {"replica": lax.rem(zi + d, 4) * 2 + yi}
        return copy_to(ref, ref, hs_sem.at[n, 4 + d], hr_sem.at[n, 4 + d], where)

    def along_y(n, d, y):
        dst = slot_ref(n, slot_of(d, y))
        return copy_to(pieces_of[n][0] if d == 0 else dst, dst, ys_sem.at[n, d], yr_sem.at[n, d], y_mate)

    def keep_piece(n):
        return pltpu.make_async_copy(pieces_of[n][0], slot_ref(n, rep), out_sem.at[n])

    def share_start(n):
        along_y(n, 0, yi).start()
        for d in (1, 3, 2):
            along_z(n, d, rep).start()
        keep_piece(n).start()

    def share_on(n):
        if n in (2, 3):
            along_y(n, 0, 1 - yi).wait_recv()
            for d in (1, 3, 2):
                along_z_late(n, d, flip(rep)).start()
            return
        for d in (1, 3, 2):
            along_z(n, d, slot_of(d, yi)).wait_recv()
            along_y(n, d, yi).start()

    for j in range(1, REPL):
        vec_copy(j).start()
    cross_copy(0).wait_recv()
    pm[...] = (em[sec, :64] + ym[:64].astype(F32)).astype(BF16)
    p2[...] = (em[sec, 64:] + ym[64:].astype(F32)).astype(BF16)
    turn_start(0)
    share_start(3)
    turn_wait(0)
    share_start(0)
    total = vg_o[...]
    for j in range(1, REPL):
        vec_copy(j).wait_recv()
        total = total + lv[j]
    vg_o_sum = total
    zv[...] = jnp.where(sec == 0, vg_o_sum[1], vg_o_sum[0])
    cross_copy(3).start()
    share_on(3)
    collect_att(0)
    za[...] = ea[1 - sec].astype(BF16)
    zc[...] = ec[1 - sec].astype(BF16)
    cross_copy(1).start()
    cross_copy(2).start()
    cross_copy(3).wait_recv()
    tv[...] = jnp.where(sec == 0, vg_o_sum[0], vg_o_sum[1]) + yv[...]
    fv[me] = tv[...]
    for j in range(1, REPL):
        vec_share(j, me).start()
    cross_copy(1).wait_recv()
    cross_copy(2).wait_recv()
    pa[...] = (ea[sec] + ya[...].astype(F32)).astype(BF16)
    pc[...] = (ec[sec] + yc[...].astype(F32)).astype(BF16)
    turn_start(1)
    share_start(2)
    turn_wait(1)
    for t in range(3):
        for chip in range(CHIPS):
            at = t * D + chip * WO
            qa[:, at : at + WO] = qt[chip * 16 : chip * 16 + 16, t * WO : t * WO + WO]
    share_start(1)
    share_on(0)
    share_on(2)
    share_on(1)
    for n in range(4):
        if n in (2, 3):
            for d in (1, 3, 2):
                along_z(n, d, slot_of(d, yi)).wait_recv()
                along_z_late(n, d, slot_of(d, 1 - yi)).wait_recv()
        else:
            for d in range(4):
                along_y(n, d, 1 - yi).wait_recv()
        keep_piece(n).wait()
    for j in range(1, REPL):
        vec_share(j, lax.rem(me + 8 - j, 8)).wait_recv()
    total = fv[0]
    for n in range(1, 8):
        total = total + fv[n]
    zv_sum[...] = total
    mine = pl.ds(pl.multiple_of(me * 128, 128), 128)
    for row, k in ((0, 0), (1, 1), (4, 3), (5, 4), (6, 5), (11, 7)):
        vo[row : row + 1, :] = zv_sum[k : k + 1, mine]
    for row, k, chip, base, t in [(2, 2, lax.rem(me, 4), me // 4 * 256, t) for t in range(2)] + [
        (7, 6, x, c * 512, t) for t in range(4)
    ]:
        cols = pl.ds(pl.multiple_of(base + t * 128, 128), 128)
        vo[row + t : row + t + 1, :] = fv[2 * chip, k : k + 1, cols] + fv[2 * chip + 1, k : k + 1, cols]

    carry_copy.wait_recv()
    edge_o[1 - sec] = carry_r[...].astype(F32)
    carry_copy.wait_send()
    swap_copy.wait_send()
    for kind in kinds:
        for d in kinds[kind]:
            if d != 0:
                x_copy(kind, d, x).wait_send()
            near_copy(kind, d, c).wait_send()
            across_copy(kind, d, sec, yi).wait_send()
            if kind != 0:
                pass_copy(kind, d, 1 - yi).wait_send()
            far_copy(kind, d, c).wait_send()
    for l in range(2):
        for d in (1, 2, 3):
            for buf, kind in ((n1, AG1), (n2, AG2), (g, BAG1), (ga, BAG2)):
                gather_copy(buf, kind, l, d, x).wait_send()
        for d in range(CHIPS):
            kv_copy(l, d).wait_send()
        dkv_copy(l).wait_send()
    each_piece(0, (0, 1, 2, 3), sent)
    for cp in pair_mlp(0) + pair_att(0):
        cp.wait_send()
    for n in range(4):
        cross_copy(n).wait_send()
    for n in range(2):
        for d in (1, 2, 3):
            turn_copy(n, d, x).wait_send()
    for n in range(4):
        for d in (1, 2, 3):
            along_z(n, d, rep).wait_send()
            if n in (2, 3):
                along_z_late(n, d, flip(rep)).wait_send()
        for d in range(1 if n in (2, 3) else 4):
            along_y(n, d, yi).wait_send()
    for j in range(1, REPL):
        vec_copy(j).wait_send()
        vec_share(j, me).wait_send()


def run_step(*operands):
    vm = pl.BlockSpec(memory_space=pltpu.VMEM)
    hbm = pl.BlockSpec(memory_space=pl.ANY)
    sds = jax.ShapeDtypeStruct
    dma = pltpu.SemaphoreType.DMA
    return pl.pallas_call(
        step_kernel,
        out_shape=(
            sds((MICRO, ROWS, D), F32),
            sds((16, 128), F32),
            sds((128, FF), BF16),
            sds((128, 3 * D), BF16),
            sds((128, D), BF16),
            sds((512, D), BF16),
        ),
        in_specs=[vm] * 10 + [hbm] * 4,
        out_specs=(vm, vm, hbm, hbm, hbm, hbm),
        scratch_shapes=[
            pltpu.VMEM((8, 8, D), F32),
            pltpu.VMEM((KEYS, 128), jnp.int32),
            pltpu.VMEM((16, 128), F32),
            pltpu.VMEM((2, 8, 16, 128), F32),
            pltpu.VMEM((2, D, WQ), BF16),
            pltpu.VMEM((2, WO, D), BF16),
            pltpu.VMEM((2, D, W1), BF16),
            pltpu.VMEM((2, W1, D), BF16),
            pltpu.VMEM((2, TOK, D), BF16),
            pltpu.VMEM((2, TOK, D), BF16),
            pltpu.VMEM((2, TOK, W1), BF16),
            pltpu.VMEM((2, TOK, W1), F32),
            pltpu.VMEM((2, TOK, WQ), BF16),
            pltpu.VMEM((2, TOK, 2 * WO), BF16),
            pltpu.VMEM((2, TOK, WO), BF16),
            pltpu.VMEM((2, ROWS, D), F32),
            pltpu.VMEM((2, ROWS, D), F32),
            pltpu.VMEM((2, TOK, D), BF16),
            pltpu.VMEM((2, TOK, D), BF16),
            pltpu.VMEM((2, TOK, W1), BF16),
            pltpu.VMEM((2, TOK, WQ), BF16),
            pltpu.VMEM((TOK, WO), BF16),
            pltpu.VMEM((3, ROWS, D), BF16),
            pltpu.VMEM((4, 3, ROWS, D), BF16),
            pltpu.VMEM((ROWS, D), BF16),
            pltpu.VMEM((ROWS, D), BF16),
            pltpu.VMEM((ROWS, D), BF16),
            pltpu.VMEM((KEYS, 2 * WO), F32),
            pltpu.VMEM((2, TOK, 2 * WO), BF16),
            pltpu.VMEM((2, TOK, 2 * WO), BF16),
            pltpu.VMEM((ROWS, D), F32),
            pltpu.VMEM((ROWS, D), F32),
            pltpu.VMEM((CHIPS, 2, 128, WQ), BF16),
            pltpu.VMEM((CHIPS, 2, 128, W1), BF16),
            pltpu.VMEM((2, 128, D), BF16),
            pltpu.VMEM((2, 512, D), BF16),
            pltpu.VMEM((CHIPS, 128, WQ), BF16),
            pltpu.VMEM((CHIPS, 128, W1), BF16),
            pltpu.VMEM((128, D), BF16),
            pltpu.VMEM((512, D), BF16),
            pltpu.VMEM((2, REPL, CHIPS, 16, WQ), BF16),
            pltpu.VMEM((2, REPL, CHIPS, 16, W1), BF16),
            pltpu.VMEM((2, REPL, 16, D), BF16),
            pltpu.VMEM((2, REPL, 64, D), BF16),
            pltpu.VMEM((2, 8, D), F32),
            pltpu.VMEM((2, 128, D), F32),
            pltpu.VMEM((2, 64, WQ), F32),
            pltpu.VMEM((2, 16, D), F32),
            pltpu.VMEM((128, D), BF16),
            pltpu.VMEM((64, WQ), BF16),
            pltpu.VMEM((16, D), BF16),
            pltpu.VMEM((128, D), BF16),
            pltpu.VMEM((64, WQ), BF16),
            pltpu.VMEM((16, D), BF16),
            pltpu.VMEM((64, D), BF16),
            pltpu.VMEM((64, D), BF16),
            pltpu.VMEM((64, WQ), BF16),
            pltpu.VMEM((16, D), BF16),
            pltpu.VMEM((16, FF), BF16),
            pltpu.VMEM((64, WQ), BF16),
            pltpu.VMEM((16, 3 * D), BF16),
            pltpu.VMEM((REPL, 2, 8, D), F32),
            pltpu.VMEM((8, D), F32),
            pltpu.VMEM((8, D), F32),
            pltpu.VMEM((8, D), F32),
            pltpu.VMEM((8, D), F32),
            dma((8, 2, CHIPS)),
            dma((8, 2, CHIPS)),
            dma((2, CHIPS)),
            dma((2, CHIPS)),
            dma((2,)),
            dma((2,)),
            dma((2,)),
            dma((2,)),
            dma((7, CHIPS)),
            dma((7, CHIPS)),
            dma((7, CHIPS)),
            dma((7, CHIPS)),
            dma((7, CHIPS)),
            dma((7, CHIPS)),
            dma((7, CHIPS)),
            dma((7, CHIPS)),
            dma((7, CHIPS)),
            dma((7, CHIPS)),
            dma((7,)),
            dma((2, 4)),
            dma((2, 4)),
            dma((2, 4, REPL)),
            dma((2, 4, REPL)),
            dma((4,)),
            dma((4,)),
            dma((4,)),
            dma((2, CHIPS)),
            dma((2, CHIPS)),
            dma((4, 8)),
            dma((4, 8)),
            dma((4, 4)),
            dma((4, 4)),
            dma((REPL,)),
            dma((REPL,)),
            dma((REPL,)),
            dma((REPL,)),
        ],
        compiler_params=pltpu.CompilerParams(
            collective_id=0, has_side_effects=True, vmem_limit_bytes=63 * 1024 * 1024
        ),
    )(*operands)


def body(
    boundary, image_of_token, ln1_gain, ln1_bias, w_qkv, qv_bias, w_out, out_bias,
    ln2_gain, ln2_bias, w_fc1, fc1_bias, w_fc2, fc2_bias,
):
    me = lax.axis_index("shard")
    x, c = me // 2, me % 2
    sec = lax.axis_index("section")
    bnd = boundary[0, :, 0]
    ids = lax.dynamic_index_in_dim(image_of_token[:, 0], sec, 0, keepdims=False).reshape(CHIPS, 2, ROWS)
    flipped = jnp.where(c == 0, ids, ids[:, ::-1])
    ids = jnp.swapaxes(flipped, 0, 1).reshape(KEYS)
    idr = jnp.broadcast_to(ids[None, :], (8, KEYS))
    edge, vo, f1, fa, fc, f2 = run_step(
        bnd, idr, ln1_gain, ln1_bias, qv_bias, out_bias, ln2_gain, ln2_bias, fc1_bias, fc2_bias,
        w_qkv[0], w_out[0], w_fc1[0], w_fc2[0],
    )
    g_qkv, g_fc1, g_out, g_fc2 = (v.astype(F32) for v in (fa, f1, fc, f2))

    def part(at, count):
        return vo[at : at + count].reshape(1, count * 128)

    return (
        edge[None, :, None],
        part(0, 1),
        part(1, 1),
        g_qkv[None],
        part(2, 2),
        g_out[None],
        part(4, 1),
        part(5, 1),
        part(6, 1),
        g_fc1[None],
        part(7, 4),
        g_fc2[None],
        part(11, 1),
    )


def solution(mesh):
    row = P("section", "shard")
    mat = P("section", "shard", None)
    edge = P("section", None, "replica", "shard", None)
    in_specs = (edge, P(None, "replica", None), row, row, mat, row, mat, row, row, row, mat, row, mat, row)
    out_specs = (edge, row, row, mat, row, mat, row, row, row, mat, row, mat, row)
    return jax.shard_map(body, mesh=mesh, in_specs=in_specs, out_specs=out_specs, check_vma=False)
```
